32 devices in a mesh: dp: 16 (over z, y, core), seq: 2 (over x).
Axes of the slice: x: 2, y: 2, z: 4, core: 2. Of those that a mesh axis runs over, the one named last changes fastest.
Arguments:
- queries: bfloat16 [16, 256, 2048], P('dp', 'seq'), may hold values from -6 to 6
- keys: bfloat16 [16, 256, 2048], P('dp', 'seq'), may hold values from -6 to 6
- values: bfloat16 [16, 256, 2048], P('dp', 'seq'), may hold values from -6 to 6
- decay_bias: float32 [16, 16, 256], P('dp', None, 'seq'), may hold values from -14 to -1
- gate_matrix: bfloat16 [6144, 16], replicated, may hold values from -0.078125 to 0.078125
- resets: int32 [16, 2], P('dp', 'seq'), may hold values 0 or 1
- cotangent: bfloat16 [16, 256, 2048], P('dp', 'seq'), may hold values from -6 to 6
Outputs:
- output: bfloat16 [16, 256, 2048], P('dp', 'seq')
- grad_queries: bfloat16 [16, 256, 2048], P('dp', 'seq')
- grad_keys: bfloat16 [16, 256, 2048], P('dp', 'seq')
- grad_values: bfloat16 [16, 256, 2048], P('dp', 'seq')
- grad_gate: float32 [6144, 16], P(('dp', 'seq'))
The draws below stay inside these ranges and needn't reach their ends.
All inputs are finite; a program needn't handle non-finite values. No bound on the sum of `resets` on one device may be relied on, other than what follows from the above.
Results may differ from the reference program's by a relative error of at most 0.012.
Values may be sent and summed in bfloat16 or wider, within the bound.
No kernel may reach another device: no remote copies, remote signals or barrier semaphores. Data moves between devices by JAX's collectives and lax.ppermute only.
A program may use at most 64 MiB of HBM per device.

```python
import jax
import jax.numpy as jnp
from jax import lax

HEADS = 16
HEAD_DIM = 128
BLOCK = 128
TOK_DEV = 128
PACKED_TOTAL = 16
WINDOW_TOKENS = 256
BLOCKS = 2
WIDTH = 2048
GATE_IN = 6144


def draw_decay_bias(key, part):
    pick_key = jax.random.fold_in(key, 11)
    slow_key = jax.random.fold_in(key, 12)
    quick_key = jax.random.fold_in(key, 13)
    shift_key = jax.random.fold_in(key, 14)
    spike_prng_seed = jax.random.fold_in(key, 15)
    fast_share = 0.5
    chosen = jax.random.uniform(pick_key, (PACKED_TOTAL, HEADS, 1)) < fast_share
    gradual_frequencies = jnp.log(jax.random.uniform(slow_key, (PACKED_TOTAL, HEADS, 1), minval=0.05, maxval=0.4) / WINDOW_TOKENS) - 0.5
    quick_rates = jnp.log(jax.random.uniform(quick_key, (PACKED_TOTAL, HEADS, 1), minval=1.0 / 50.0, maxval=1.0 / 30.0)) - 0.5
    default_frequencies = jnp.where(chosen, quick_rates, gradual_frequencies)
    portion_shift = jax.random.uniform(shift_key, (PACKED_TOTAL, 1, WINDOW_TOKENS // TOK_DEV), minval=-0.7, maxval=0.7)
    portion_shift = jnp.repeat(portion_shift, TOK_DEV, axis=2)
    spike_occurrences = jax.random.bernoulli(spike_prng_seed, 3.0 / WINDOW_TOKENS, (PACKED_TOTAL, 1, WINDOW_TOKENS))
    return jnp.where(spike_occurrences, -1.2, default_frequencies + portion_shift).astype(jnp.float32)


def place_ends(array, rng, smallest, top_value):
    dims = array.shape
    spot = [jax.random.randint(jax.random.fold_in(rng, axis), (), 0, dims[axis]) for axis in range(len(dims))]
    array = array.at[tuple(spot)].set(smallest)
    longest = dims.index(max(dims))
    spot[longest] = (spot[longest] + 1) % dims[longest]
    return array.at[tuple(spot)].set(top_value)


def block_levels(own_key, extent, cuts, least, largest):
    level, own = 1.0, jax.random.fold_in(own_key, 6)
    for position, blocks in cuts:
        draws = jnp.exp(jax.random.uniform(jax.random.fold_in(own, position), (blocks,), jnp.float32, least / len(cuts), largest / len(cuts)))
        level = level * jnp.repeat(draws, extent[position] // blocks).reshape([-1 if axis == position else 1 for axis in range(len(extent))])
    return level


def noise(key, extent, scale, most, shards=(), kind=jnp.bfloat16):
    loudness = block_levels(key, extent, shards, -0.22, 0.18) if shards else 1.0
    result = jax.random.normal(key, extent, jnp.float32) * scale * loudness
    return jnp.minimum(jnp.maximum(result, -most), most).astype(kind)


def setup_inputs(seed: int = 0) -> dict:
    splits = jax.random.split(jax.random.key(seed), 8)
    queries = noise(splits[0], (PACKED_TOTAL, WINDOW_TOKENS, WIDTH), 1.0, 6.0, ((0, 16), (1, 2)))
    keys = noise(splits[1], (PACKED_TOTAL, WINDOW_TOKENS, WIDTH), 1.0, 6.0, ((0, 16), (1, 2)))
    values = noise(splits[2], (PACKED_TOTAL, WINDOW_TOKENS, WIDTH), 1.0, 6.0, ((0, 16), (1, 2)))
    decay_bias = draw_decay_bias(jax.random.fold_in(splits[7], 71), 0)
    gate_matrix = noise(splits[4], (GATE_IN, HEADS), GATE_IN ** -0.5, 0.078125)
    resets = place_ends((jax.random.randint(splits[5], (PACKED_TOTAL, BLOCKS), 0, 3) < 1).astype(jnp.int32), jax.random.fold_in(splits[5], 1), 0, 1)
    cotangent = noise(splits[6], (PACKED_TOTAL, WINDOW_TOKENS, WIDTH), 1.0, 6.0, ((0, 16), (1, 2)))
    return dict(queries=queries, keys=keys, values=values, decay_bias=decay_bias, gate_matrix=gate_matrix, resets=resets, cotangent=cotangent)


EPSILON = 1e-06

def one_sequence(queries, keys, values, bias_rows, resets, cotangent, gate_matrix):
    model_width = HEADS * HEAD_DIM
    shape_four = (BLOCKS, BLOCK, HEADS, HEAD_DIM)
    query_blocks = queries.reshape(shape_four).astype(jnp.float32)
    key_blocks = keys.reshape(shape_four).astype(jnp.float32)
    value_blocks = values.reshape(shape_four).astype(jnp.float32)
    joined = jnp.concatenate([queries, keys, values], axis=1)
    logits = jnp.dot(joined, gate_matrix, preferred_element_type=jnp.float32) + bias_rows.T
    logdecay = -jax.nn.softplus(logits)
    cumulative = jnp.cumsum(logdecay.reshape(BLOCKS, BLOCK, HEADS), axis=1)
    totals = cumulative[:, -1, :]
    kept_flags = (1 - resets).astype(jnp.float32)
    factors = kept_flags[:, None] * jnp.exp(totals)
    fading = jnp.exp(totals[:, None, :] - cumulative)
    decayed_keys = (fading[..., None] * key_blocks).astype(jnp.bfloat16)
    updates = jnp.einsum('nche,nchf->nhef', decayed_keys.astype(jnp.float32), value_blocks)

    def advance(carried_state, element):
        factor_row, flag_row, update_row = element
        return (factor_row[:, None, None] * carried_state + update_row, flag_row * carried_state)
    zero_state = jnp.zeros((HEADS, HEAD_DIM, HEAD_DIM), jnp.float32)
    _, entering = lax.scan(advance, zero_state, (factors, kept_flags, updates))
    ending = jnp.exp(totals)[:, :, None, None] * entering + updates
    scores = jnp.einsum('nthe,nshe->nhts', query_blocks, key_blocks)
    cum_heads = jnp.transpose(cumulative, (0, 2, 1))
    lower_mask = jnp.tril(jnp.ones((BLOCK, BLOCK), dtype=bool))
    differences = cum_heads[:, :, :, None] - cum_heads[:, :, None, :]
    decays = jnp.exp(jnp.where(lower_mask, differences, -jnp.inf))
    attn = decays * scores
    attn_b = attn.astype(jnp.bfloat16)
    within = jnp.einsum('nhts,nshf->nthf', attn_b.astype(jnp.float32), value_blocks)
    entering_b = entering.astype(jnp.bfloat16)
    carried = jnp.exp(cumulative)[..., None] * jnp.einsum('nthe,nhef->nthf', query_blocks, entering_b.astype(jnp.float32))
    mixture = within + carried
    norm_root = jnp.sqrt(lax.optimization_barrier(jnp.mean(mixture * mixture, axis=-1, keepdims=True)) + EPSILON)
    normed = mixture / norm_root
    output = normed.astype(jnp.bfloat16).reshape(WINDOW_TOKENS, model_width)
    upstream = cotangent.reshape(shape_four).astype(jnp.float32)
    d_mixture = (upstream - normed * lax.optimization_barrier(jnp.mean(upstream * normed, axis=-1, keepdims=True))) / norm_root
    d_mixture_b = d_mixture.astype(jnp.bfloat16)
    d_mix_wide = d_mixture_b.astype(jnp.float32)
    d_attn = jnp.einsum('nthf,nshf->nhts', d_mix_wide, value_blocks)
    weighted = (decays * d_attn).astype(jnp.bfloat16).astype(jnp.float32)
    q_decay = (jnp.exp(cumulative)[..., None] * query_blocks).astype(jnp.bfloat16)
    local_grad = jnp.einsum('nthe,nthf->nhef', q_decay.astype(jnp.float32), d_mix_wide)
    pushed = kept_flags[:, None, None, None] * local_grad

    def retreat(carried_grad, element):
        factor_row, pushed_row = element
        return (factor_row[:, None, None] * carried_grad + pushed_row, carried_grad)
    _, state_grads = lax.scan(retreat, zero_state, (factors, pushed), reverse=True)
    state_grads_b = state_grads.astype(jnp.bfloat16).astype(jnp.float32)
    from_state = fading[..., None] * jnp.einsum('nthf,nhef->nthe', value_blocks, state_grads_b)
    products = attn * d_attn
    d_cumul = jnp.transpose(lax.optimization_barrier(jnp.sum(products, axis=3)) - lax.optimization_barrier(jnp.sum(products, axis=2)), (0, 2, 1))
    d_cumul = d_cumul + lax.optimization_barrier(jnp.sum(d_mixture * carried, axis=-1)) - lax.optimization_barrier(jnp.sum(key_blocks * from_state, axis=-1))
    d_cumul = d_cumul.at[:, -1, :].add(lax.optimization_barrier(jnp.sum(state_grads * ending, axis=(2, 3))))
    d_logdecay = jnp.cumsum(d_cumul[:, ::-1, :], axis=1)[:, ::-1, :]
    d_logits = (-jax.nn.sigmoid(logits) * d_logdecay.reshape(WINDOW_TOKENS, HEADS)).astype(jnp.bfloat16)
    gate_back = jnp.dot(d_logits, gate_matrix.T, preferred_element_type=jnp.float32)
    grad_q = jnp.einsum('nhts,nshe->nthe', weighted, key_blocks)
    grad_q = grad_q + jnp.exp(cumulative)[..., None] * jnp.einsum('nthf,nhef->nthe', d_mix_wide, entering_b.astype(jnp.float32))
    grad_k = jnp.einsum('nhts,nthe->nshe', weighted, query_blocks) + from_state
    grad_v = jnp.einsum('nhts,nthf->nshf', attn_b.astype(jnp.float32), d_mix_wide)
    grad_v = grad_v + fading[..., None] * jnp.einsum('nthe,nhef->nthf', key_blocks, state_grads_b)
    grad_q = (grad_q.reshape(WINDOW_TOKENS, model_width) + gate_back[:, :model_width]).astype(jnp.bfloat16)
    grad_k = (grad_k.reshape(WINDOW_TOKENS, model_width) + gate_back[:, model_width:2 * model_width]).astype(jnp.bfloat16)
    grad_v = (grad_v.reshape(WINDOW_TOKENS, model_width) + gate_back[:, 2 * model_width:]).astype(jnp.bfloat16)
    weight_term = jnp.dot(joined.T, d_logits, preferred_element_type=jnp.float32)
    return (output, grad_q, grad_k, grad_v, weight_term)

def reference(queries, keys, values, decay_bias, gate_matrix, resets, cotangent):

    def per_sequence(accumulated, element):
        question_vectors, key_rows, value_rows, bias_rows, reset_row, cot_rows = element
        output, grad_q, grad_k, grad_v, weight_term = one_sequence(question_vectors, key_rows, value_rows, bias_rows, reset_row, cot_rows, gate_matrix)
        return (accumulated + weight_term, (output, grad_q, grad_k, grad_v))
    starting_sum = jnp.zeros((GATE_IN, HEADS), jnp.float32)
    grad_gate, (output, grad_q, grad_k, grad_v) = lax.scan(per_sequence, starting_sum, (queries, keys, values, decay_bias, resets, cotangent))
    return (output, grad_q, grad_k, grad_v, grad_gate)
```

```python
import functools

import jax
import jax.numpy as jnp
from jax import lax
from jax.experimental import pallas as pl
from jax.experimental.pallas import tpu as pltpu
from jax.sharding import PartitionSpec as P

EPSILON = 1e-06
F32 = jnp.float32
BF16 = jnp.bfloat16
VMEM_LIMIT = 32 * 1024 * 1024


def dot_nn(a, b):
    return lax.dot_general(a, b, (((1,), (0,)), ((), ())), preferred_element_type=F32)


def dot_nt(a, b):
    return lax.dot_general(a, b, (((1,), (1,)), ((), ())), preferred_element_type=F32)


def dot_tn(a, b):
    return lax.dot_general(a, b, (((0,), (0,)), ((), ())), preferred_element_type=F32)


def exact_dot(x, ones):
    rows = x.shape[0]
    high = x.astype(BF16)
    rest = x - high.astype(F32)
    middle = rest.astype(BF16)
    low = (rest - middle.astype(F32)).astype(BF16)
    parts = dot_nn(jnp.concatenate([high, middle, low], axis=0), ones)
    return parts[:rows] + parts[rows : 2 * rows] + parts[2 * rows :]


def triangle(size, upper):
    rows = lax.broadcasted_iota(jnp.int32, (size, size), 0)
    columns = lax.broadcasted_iota(jnp.int32, (size, size), 1)
    keep = rows <= columns if upper else rows >= columns
    return jnp.where(keep, 1.0, 0.0).astype(BF16)


def decay_matrix(cum_column, cum_row):
    size = cum_row.shape[1]
    rows = lax.broadcasted_iota(jnp.int32, (size, size), 0)
    columns = lax.broadcasted_iota(jnp.int32, (size, size), 1)
    return jnp.exp(jnp.where(columns <= rows, cum_column - cum_row, -jnp.inf))


def spec():
    return pl.BlockSpec(memory_space=pltpu.VMEM)


def smem():
    return pl.BlockSpec(memory_space=pltpu.SMEM)


def lanes(rows, width, index):
    return pl.BlockSpec((rows, width), lambda i: (0, index))


def heads_block(count, size, index):
    return pl.BlockSpec((count, size, size), lambda i: (index, 0, 0))


def params():
    return pltpu.CompilerParams(vmem_limit_bytes=VMEM_LIMIT)


def gate_kernel(heads, q, k, v, bias, gate, logits_ref, cum_ref, updates_ref):
    width = q.shape[1]
    size = width // heads
    logits = (
        dot_nt(gate[:, :width], q[...])
        + dot_nt(gate[:, width : 2 * width], k[...])
        + dot_nt(gate[:, 2 * width :], v[...])
        + bias[...]
    )
    logits_ref[...] = logits
    soft = jnp.maximum(logits, 0.0) + jnp.log1p(jnp.exp(-jnp.abs(logits)))
    tokens = logits.shape[1]
    cum = exact_dot(-soft, triangle(tokens, True))
    cum_ref[...] = cum
    fading = jnp.exp(cum[:, tokens - 1 :] - cum)
    for h in range(heads):
        part = slice(h * size, (h + 1) * size)
        faded = (k[:, part].astype(F32).T * fading[h : h + 1, :]).astype(BF16)
        updates_ref[h] = dot_nn(faded, v[:, part]).astype(BF16)


def mix_kernel(first, count, q, k, v, cot, cum_ref, state, resets, out, d_mix, pushed, row_ref):
    size = state.shape[1]
    kept = (1 - resets[0, 0]).astype(F32)
    cum_columns = cum_ref[...].T
    row_terms = []
    for i in range(count):
        h = first + i
        part = slice(i * size, (i + 1) * size)
        q_h, v_h = q[:, part], v[:, part]
        column, row = cum_columns[:, h : h + 1], cum_ref[h : h + 1, :]
        attn = (decay_matrix(column, row) * dot_nt(q_h, k[:, part])).astype(BF16)
        carried = (kept * jnp.exp(column)) * dot_nn(q_h, state[i])
        mixture = dot_nn(attn, v_h) + carried
        square = jnp.mean(mixture * mixture, axis=1, keepdims=True) + EPSILON
        inverse = lax.rsqrt(square)
        normed = mixture * inverse
        out[:, part] = normed.astype(BF16)
        upstream = cot[:, part].astype(F32)
        along = jnp.mean(upstream * normed, axis=1, keepdims=True)
        d_h = ((upstream - normed * along) * inverse).astype(BF16)
        d_mix[:, part] = d_h
        row_terms.append(along * (size * EPSILON) * (inverse * inverse))
        faded = (q_h.astype(F32).T * (kept * jnp.exp(row))).astype(BF16)
        pushed[i] = dot_nn(faded, d_h).astype(BF16)
    row_ref[...] = jnp.concatenate(row_terms, axis=1)


def back_kernel(heads, q, k, v, d_mix, cum_ref, state, resets, gq, gk, gv, column_ref):
    size = state.shape[1]
    kept = (1 - resets[0, 0]).astype(F32)
    cum_columns = cum_ref[...].T
    sums = []
    for h in range(heads):
        part = slice(h * size, (h + 1) * size)
        q_h, k_h, v_h, d_h = q[:, part], k[:, part], v[:, part], d_mix[:, part]
        column, row = cum_columns[:, h : h + 1], cum_ref[h : h + 1, :]
        decays = decay_matrix(column, row)
        attn = (decays * dot_nt(q_h, k_h)).astype(BF16)
        weighted = (decays * dot_nt(d_h, v_h)).astype(BF16)
        gq[:, part] = dot_nn(weighted, k_h) + (kept * jnp.exp(column)) * dot_nt(d_h, state[h])
        gk_h = dot_tn(weighted, q_h)
        gk[:, part] = gk_h
        gv[:, part] = dot_tn(attn, d_h)
        sums.append(jnp.sum(k_h.astype(F32) * gk_h, axis=1, keepdims=True))
    column_ref[...] = jnp.concatenate(sums, axis=1)


def logit_kernel(
    heads, order, q, k, v, cum_ref, logits_ref, grads, terms, through, place, d_ref, *outs
):
    size = grads.shape[1]
    width = q.shape[1]
    cum = cum_ref[...]
    tokens = cum.shape[1]
    totals = cum[:, tokens - 1 :]
    sums = []
    for h in range(heads):
        part = slice(h * size, (h + 1) * size)
        sums.append(
            jnp.sum(k[:, part].astype(F32) * dot_nt(v[:, part], grads[h]), axis=1, keepdims=True)
        )
    from_state = jnp.concatenate(sums, axis=1).T * jnp.exp(totals - cum)
    ends = jnp.sum(from_state, axis=1, keepdims=True) + jnp.exp(totals) * through[...]
    last = lax.broadcasted_iota(jnp.int32, cum.shape, 1) == tokens - 1
    d_cum = terms[...].T - from_state + jnp.where(last, ends, 0.0)
    d_decay = exact_dot(d_cum, triangle(tokens, False))
    d_logits = (-jax.nn.sigmoid(logits_ref[...]) * d_decay).astype(BF16)
    d_ref[...] = d_logits
    arrays = (q, k, v)
    if order is None:
        for i in range(3):
            outs[0][:, i * width : (i + 1) * width] = dot_nn(d_logits, arrays[i][...])
        return
    chunks = 2 * outs[0].shape[0]
    share = outs[0].shape[2]
    whole = [dot_nn(d_logits, arrays[i][...]).astype(BF16) for i in range(3)]
    joined = jnp.concatenate(whole, axis=1)
    mine = place[0]
    for j in range(chunks):
        relative = mine ^ j
        position = 0
        for bit, mask in enumerate(order):
            position = position + jnp.where((relative & mask) != 0, chunks >> (bit + 1), 0)
        piece = joined[:, j * share : (j + 1) * share]

        @pl.when(position < chunks // 2)
        def _():
            outs[0][position] = piece

        @pl.when(position >= chunks // 2)
        def _():
            outs[1][position - chunks // 2] = piece


def finish_q_kernel(gq, d_logits, gate, out):
    out[...] = (gq[...] + dot_tn(d_logits[...], gate[...])).astype(BF16)


def finish_k_kernel(heads, gk, v, grads, cum_ref, d_logits, gate, out):
    size = grads.shape[1]
    cum = cum_ref[...]
    fading = jnp.exp(cum[:, cum.shape[1] - 1 :] - cum).T
    back = dot_tn(d_logits[...], gate[...])
    for h in range(heads):
        part = slice(h * size, (h + 1) * size)
        state_part = fading[:, h : h + 1] * dot_nt(v[:, part], grads[h])
        out[:, part] = (gk[:, part] + state_part + back[:, part]).astype(BF16)


def finish_v_kernel(heads, gv, k, grads, cum_ref, d_logits, gate, out):
    size = grads.shape[1]
    cum = cum_ref[...]
    fading = jnp.exp(cum[:, cum.shape[1] - 1 :] - cum).T
    back = dot_tn(d_logits[...], gate[...])
    for h in range(heads):
        part = slice(h * size, (h + 1) * size)
        state_part = fading[:, h : h + 1] * dot_nn(k[:, part], grads[h])
        out[:, part] = (gv[:, part] + state_part + back[:, part]).astype(BF16)


def shape(dims, dtype):
    return jax.ShapeDtypeStruct(dims, dtype)


GROUPS = 4


def body(dp_size, seq_size, queries, keys, values, decay_bias, gate_matrix, resets, cotangent):
    q, k, v, cot = queries[0], keys[0], values[0], cotangent[0]
    tokens, width = q.shape
    heads = decay_bias.shape[1]
    size = width // heads
    gate = gate_matrix.T
    forward = [(i, i + 1) for i in range(seq_size - 1)]
    backward = [(i + 1, i) for i in range(seq_size - 1)]
    kept = (1 - resets[0, 0]).astype(F32)

    logits, cum, updates = pl.pallas_call(
        functools.partial(gate_kernel, heads),
        out_shape=(
            shape((heads, tokens), F32),
            shape((heads, tokens), F32),
            shape((heads, size, size), BF16),
        ),
        in_specs=[spec()] * 5,
        out_specs=(spec(),) * 3,
        compiler_params=params(),
        name="gate",
    )(q, k, v, decay_bias[0], gate)
    totals = jnp.exp(cum[:, -1])[:, None, None]

    count = heads // GROUPS
    entering, outs, d_mixes, pushed, rows = [], [], [], [], []
    for g in range(GROUPS):
        own = updates[g * count : (g + 1) * count]
        arrived = lax.ppermute(own, "seq", forward)
        for _ in range(seq_size - 2):
            factor = kept * totals[g * count : (g + 1) * count]
            ending = factor * arrived.astype(F32) + own.astype(F32)
            arrived = lax.ppermute(ending.astype(BF16), "seq", forward)
        entering.append(arrived)
    state_grads = []
    for g in range(GROUPS):
        out_g, d_g, pushed_g, rows_g = pl.pallas_call(
            functools.partial(mix_kernel, g * count, count),
            grid=(1,),
            out_shape=(
                shape((tokens, count * size), BF16),
                shape((tokens, count * size), BF16),
                shape((count, size, size), BF16),
                shape((tokens, count), F32),
            ),
            in_specs=[lanes(tokens, count * size, g)] * 4 + [spec(), spec(), smem()],
            out_specs=(spec(),) * 4,
            compiler_params=params(),
            name="mix",
        )(q, k, v, cot, cum, entering[g], resets)
        outs.append(out_g)
        d_mixes.append(d_g)
        rows.append(rows_g)
        arrived = lax.ppermute(pushed_g, "seq", backward)
        for _ in range(seq_size - 2):
            factor = kept * totals[g * count : (g + 1) * count]
            total = factor * arrived.astype(F32) + pushed_g.astype(F32)
            arrived = lax.ppermute(total.astype(BF16), "seq", backward)
        state_grads.append(arrived)
    output = jnp.concatenate(outs, axis=1)
    d_mix = jnp.concatenate(d_mixes, axis=1)
    state = jnp.concatenate(entering, axis=0)
    grads = jnp.concatenate(state_grads, axis=0)

    gq, gk, gv, columns = pl.pallas_call(
        functools.partial(back_kernel, heads),
        out_shape=(
            shape((tokens, width), F32),
            shape((tokens, width), F32),
            shape((tokens, width), F32),
            shape((tokens, heads), F32),
        ),
        in_specs=[spec()] * 6 + [smem()],
        out_specs=(spec(),) * 4,
        compiler_params=params(),
        name="back",
    )(q, k, v, d_mix, cum, state, resets)
    terms = jnp.concatenate(rows, axis=1) - columns
    if seq_size > 2:
        through = kept * jnp.sum(grads.astype(F32) * state.astype(F32), axis=(1, 2))[:, None]
    else:
        through = jnp.zeros((heads, 1), F32)

    share = 3 * width // dp_size
    halving = (
        dp_size > 1 and dp_size & (dp_size - 1) == 0 and share % 128 == 0 and seq_size == 2
    )
    order = [1 << b for b in range(dp_size.bit_length() - 1)] if halving else None
    if halving:
        part_shapes = (shape((dp_size // 2, heads, share), BF16),) * 2
    else:
        part_shapes = (shape((heads, 3 * width), F32),)
    place = lax.axis_index("dp").astype(jnp.int32).reshape(1)
    d_logits, *parts = pl.pallas_call(
        functools.partial(logit_kernel, heads, order),
        out_shape=(shape((heads, tokens), BF16),) + part_shapes,
        in_specs=[spec()] * 8 + [smem()],
        out_specs=(spec(),) * (1 + len(part_shapes)),
        compiler_params=params(),
        name="logits",
    )(q, k, v, cum, logits, grads, terms, through, place)

    if halving:
        keep, send = parts
        for step, mask in enumerate(order):
            arrived = lax.ppermute(send, "dp", [(i, i ^ mask) for i in range(dp_size)])
            total = keep.astype(F32) + arrived.astype(F32)
            half = total.shape[0] // 2
            if half:
                keep, send = total[:half].astype(BF16), total[half:].astype(BF16)
        total = total[0]
        arrived = lax.ppermute(total.astype(BF16), "seq", [(0, 1), (1, 0)])
        total = total + arrived.astype(F32)
        piece = share // seq_size
        grad_gate = lax.dynamic_slice_in_dim(total, lax.axis_index("seq") * piece, piece, axis=1).T
    else:
        grad_gate = lax.psum_scatter(
            parts[0].T, ("dp", "seq"), scatter_dimension=0, tiled=True
        )

    def finish(kernel, arrays, index):
        return pl.pallas_call(
            kernel,
            grid=(1,),
            out_shape=shape((tokens, width), BF16),
            in_specs=[spec()] * (len(arrays) + 1) + [lanes(heads, width, index)],
            out_specs=spec(),
            compiler_params=params(),
            name="finish",
        )(*arrays, d_logits, gate)

    grad_q = finish(finish_q_kernel, (gq,), 0)
    grad_k = finish(functools.partial(finish_k_kernel, heads), (gk, v, grads, cum), 1)
    grad_v = finish(functools.partial(finish_v_kernel, heads), (gv, k, grads, cum), 2)
    return output[None], grad_q[None], grad_k[None], grad_v[None], grad_gate


def solution(mesh):
    rows = P("dp", "seq", None)
    return jax.shard_map(
        functools.partial(body, mesh.shape["dp"], mesh.shape["seq"]),
        mesh=mesh,
        in_specs=(rows, rows, rows, P("dp", None, "seq"), P(), P("dp", "seq"), rows),
        out_specs=(rows, rows, rows, rows, P(("dp", "seq"), None)),
        check_vma=False,
    )
```

```python
import functools

import jax
import jax.numpy as jnp
from jax import lax
from jax.experimental import pallas as pl
from jax.experimental.pallas import tpu as pltpu
from jax.sharding import PartitionSpec as P

EPSILON = 1e-06
F32 = jnp.float32
BF16 = jnp.bfloat16
SMALL = 16 * 1024 * 1024
LARGE = 60 * 1024 * 1024


def dot_nn(a, b):
    return lax.dot_general(a, b, (((1,), (0,)), ((), ())), preferred_element_type=F32)


def dot_nt(a, b):
    return lax.dot_general(a, b, (((1,), (1,)), ((), ())), preferred_element_type=F32)


def dot_tn(a, b):
    return lax.dot_general(a, b, (((0,), (0,)), ((), ())), preferred_element_type=F32)


def exact_dot(x, ones):
    rows = x.shape[0]
    high = x.astype(BF16)
    rest = x - high.astype(F32)
    middle = rest.astype(BF16)
    low = (rest - middle.astype(F32)).astype(BF16)
    parts = dot_nn(jnp.concatenate([high, middle, low], axis=0), ones)
    return parts[:rows] + parts[rows : 2 * rows] + parts[2 * rows :]


def triangle(size, upper):
    rows = lax.broadcasted_iota(jnp.int32, (size, size), 0)
    columns = lax.broadcasted_iota(jnp.int32, (size, size), 1)
    keep = rows <= columns if upper else rows >= columns
    return jnp.where(keep, 1.0, 0.0).astype(BF16)


def decay_matrix(cum_column, cum_row):
    size = cum_row.shape[1]
    rows = lax.broadcasted_iota(jnp.int32, (size, size), 0)
    columns = lax.broadcasted_iota(jnp.int32, (size, size), 1)
    return jnp.exp(jnp.where(columns <= rows, cum_column - cum_row, -jnp.inf))


def spec():
    return pl.BlockSpec(memory_space=pltpu.VMEM)


def smem():
    return pl.BlockSpec(memory_space=pltpu.SMEM)


def anywhere():
    return pl.BlockSpec(memory_space=pl.ANY)


def params(limit=SMALL):
    return pltpu.CompilerParams(vmem_limit_bytes=limit)


def cost():
    return pl.CostEstimate(flops=1000, bytes_accessed=1000, transcendentals=0)


def gate_kernel(heads, groups, q_in, k_in, v_in, bias_in, gate_in, *refs):
    logits_ref, cum_ref, *updates = refs[: 2 + len(groups)]
    q, k, v, bias, gate, sems = refs[2 + len(groups) :]
    copies = [
        pltpu.make_async_copy(source, target, sems.at[i])
        for i, (source, target) in enumerate(
            ((gate_in, gate), (bias_in, bias), (k_in, k), (q_in, q), (v_in, v))
        )
    ]
    for copy in copies:
        copy.start()
    width = q.shape[1]
    size = width // heads
    copies[0].wait()
    copies[1].wait()
    copies[2].wait()
    logits = bias[...] + dot_nt(gate[:, width : 2 * width], k[...])
    copies[3].wait()
    logits = logits + dot_nt(gate[:, :width], q[...])
    copies[4].wait()
    logits = logits + dot_nt(gate[:, 2 * width :], v[...])
    logits_ref[...] = logits
    soft = jnp.maximum(logits, 0.0) + jnp.log1p(jnp.exp(-jnp.abs(logits)))
    tokens = logits.shape[1]
    cum = exact_dot(-soft, triangle(tokens, True))
    cum_ref[...] = cum
    fading = jnp.exp(cum[:, tokens - 1 :] - cum)
    for (first, count), out in zip(groups, updates):
        for i in range(count):
            h = first + i
            part = slice(h * size, (h + 1) * size)
            faded = (k[:, part].astype(F32).T * fading[h : h + 1, :]).astype(BF16)
            out[i] = dot_nn(faded, v[:, part]).astype(BF16)


def mix_kernel(first, count, q, k, v, cot, cum_ref, state, resets, out, d_mix, pushed, row_ref):
    size = state.shape[1]
    kept = (1 - resets[0, 0]).astype(F32)
    cum_columns = cum_ref[...].T
    row_terms = []
    for i in range(count):
        h = first + i
        part = slice(h * size, (h + 1) * size)
        own = slice(i * size, (i + 1) * size)
        q_h, v_h = q[:, part], v[:, part]
        column, row = cum_columns[:, h : h + 1], cum_ref[h : h + 1, :]
        attn = (decay_matrix(column, row) * dot_nt(q_h, k[:, part])).astype(BF16)
        carried = (kept * jnp.exp(column)) * dot_nn(q_h, state[i])
        mixture = dot_nn(attn, v_h) + carried
        square = jnp.mean(mixture * mixture, axis=1, keepdims=True) + EPSILON
        inverse = lax.rsqrt(square)
        normed = mixture * inverse
        out[:, own] = normed.astype(BF16)
        upstream = cot[:, part].astype(F32)
        along = jnp.mean(upstream * normed, axis=1, keepdims=True)
        d_h = ((upstream - normed * along) * inverse).astype(BF16)
        d_mix[:, own] = d_h
        row_terms.append(jnp.sum(d_h.astype(F32) * mixture, axis=1, keepdims=True))
        faded = (q_h.astype(F32).T * (kept * jnp.exp(row))).astype(BF16)
        pushed[i] = dot_nn(faded, d_h).astype(BF16)
    row_ref[...] = jnp.concatenate(row_terms, axis=1).T


def back_kernel(heads, groups, *refs):
    q, k, v, cum_ref, resets = refs[:5]
    number = len(groups)
    outs, d_mixes, states, row_terms = [refs[5 + number * i : 5 + number * (i + 1)] for i in range(4)]
    output, gq, gk, gv, term_ref = refs[5 + 4 * number :]
    size = states[0].shape[1]
    kept = (1 - resets[0, 0]).astype(F32)
    cum_columns = cum_ref[...].T
    sums = []
    for g, (first, count) in enumerate(groups):
        output[:, first * size : (first + count) * size] = outs[g][...]
        for i in range(count):
            h = first + i
            part = slice(h * size, (h + 1) * size)
            q_h, k_h, v_h = q[:, part], k[:, part], v[:, part]
            d_h = d_mixes[g][:, i * size : (i + 1) * size]
            column, row = cum_columns[:, h : h + 1], cum_ref[h : h + 1, :]
            decays = decay_matrix(column, row)
            attn = (decays * dot_nt(q_h, k_h)).astype(BF16)
            d_attn = dot_nt(d_h, v_h)
            weighted = (decays * d_attn).astype(BF16)
            sums.append(jnp.sum(attn.astype(F32) * d_attn, axis=0, keepdims=True))
            gq[:, part] = dot_nn(weighted, k_h) + (kept * jnp.exp(column)) * dot_nt(
                d_h, states[g][i]
            )
            gk[:, part] = dot_tn(weighted, q_h)
            gv[:, part] = dot_tn(attn, d_h)
    term_ref[...] = jnp.concatenate([r[...] for r in row_terms], axis=0) - jnp.concatenate(
        sums, axis=0
    )


def logit_kernel(heads, groups, order, q, k, v, cum_ref, logits_ref, terms, through, place, *refs):
    grads = refs[: len(groups)]
    d_ref, *outs = refs[len(groups) :]
    size = grads[0].shape[1]
    width = q.shape[1]
    cum = cum_ref[...]
    tokens = cum.shape[1]
    totals = cum[:, tokens - 1 :]
    sums = []
    for g, (first, count) in enumerate(groups):
        for i in range(count):
            part = slice((first + i) * size, (first + i + 1) * size)
            moved = dot_nt(v[:, part], grads[g][i])
            sums.append(jnp.sum(k[:, part].astype(F32) * moved, axis=1, keepdims=True))
    from_state = jnp.concatenate(sums, axis=1).T * jnp.exp(totals - cum)
    ends = jnp.sum(from_state, axis=1, keepdims=True) + jnp.exp(totals) * through[...]
    last = lax.broadcasted_iota(jnp.int32, cum.shape, 1) == tokens - 1
    d_cum = terms[...] - from_state + jnp.where(last, ends, 0.0)
    d_decay = exact_dot(d_cum, triangle(tokens, False))
    d_logits = (-jax.nn.sigmoid(logits_ref[...]) * d_decay).astype(BF16)
    d_ref[...] = d_logits
    arrays = (q, k, v)
    if order is None:
        for i in range(3):
            outs[0][:, i * width : (i + 1) * width] = dot_nn(d_logits, arrays[i][...])
        return
    chunks = 2 * outs[0].shape[0]
    share = outs[0].shape[2]
    whole = [dot_nn(d_logits, arrays[i][...]).astype(BF16) for i in range(3)]
    joined = jnp.concatenate(whole, axis=1)
    mine = place[0]
    for j in range(chunks):
        relative = mine ^ j
        position = 0
        for bit, mask in enumerate(order):
            position = position + jnp.where((relative & mask) != 0, chunks >> (bit + 1), 0)
        piece = joined[:, j * share : (j + 1) * share]

        @pl.when(position < chunks // 2)
        def _():
            outs[0][position] = piece

        @pl.when(position >= chunks // 2)
        def _():
            outs[1][position - chunks // 2] = piece


def finish_q_kernel(gq, d_logits, gate, out):
    width = out.shape[1]
    out[...] = (gq[...] + dot_tn(d_logits[...], gate[:, :width])).astype(BF16)


def finish_k_kernel(groups, gk, v, cum_ref, d_logits, gate, *refs):
    *grads, out = refs
    size = grads[0].shape[1]
    width = out.shape[1]
    cum = cum_ref[...]
    fading = jnp.exp(cum[:, cum.shape[1] - 1 :] - cum).T
    back = dot_tn(d_logits[...], gate[:, width : 2 * width])
    for g, (first, count) in enumerate(groups):
        for i in range(count):
            h = first + i
            part = slice(h * size, (h + 1) * size)
            state_part = fading[:, h : h + 1] * dot_nt(v[:, part], grads[g][i])
            out[:, part] = (gk[:, part] + state_part + back[:, part]).astype(BF16)


def finish_v_kernel(groups, gv, k, cum_ref, d_logits, gate, *refs):
    *grads, out = refs
    size = grads[0].shape[1]
    width = out.shape[1]
    cum = cum_ref[...]
    fading = jnp.exp(cum[:, cum.shape[1] - 1 :] - cum).T
    back = dot_tn(d_logits[...], gate[:, 2 * width :])
    for g, (first, count) in enumerate(groups):
        for i in range(count):
            h = first + i
            part = slice(h * size, (h + 1) * size)
            state_part = fading[:, h : h + 1] * dot_nn(k[:, part], grads[g][i])
            out[:, part] = (gv[:, part] + state_part + back[:, part]).astype(BF16)


def shape(dims, dtype):
    return jax.ShapeDtypeStruct(dims, dtype)


def head_groups(heads):
    parts = 3 if heads >= 3 else 1
    sizes = [heads // parts + (1 if i < heads % parts else 0) for i in range(parts)]
    return [(sum(sizes[:i]), sizes[i]) for i in range(parts)]


def body(dp_size, seq_size, queries, keys, values, decay_bias, gate_matrix, resets, cotangent):
    q, k, v, cot = queries[0], keys[0], values[0], cotangent[0]
    tokens, width = q.shape
    heads = decay_bias.shape[1]
    size = width // heads
    gate = gate_matrix.T
    groups = head_groups(heads)
    forward = [(i, i + 1) for i in range(seq_size - 1)]
    backward = [(i + 1, i) for i in range(seq_size - 1)]
    kept = (1 - resets[0, 0]).astype(F32)

    logits, cum, *updates = pl.pallas_call(
        functools.partial(gate_kernel, heads, groups),
        out_shape=(shape((heads, tokens), F32),) * 2
        + tuple(shape((count, size, size), BF16) for _, count in groups),
        in_specs=[anywhere()] * 5,
        out_specs=(spec(),) * (2 + len(groups)),
        scratch_shapes=[
            pltpu.VMEM((tokens, width), BF16),
            pltpu.VMEM((tokens, width), BF16),
            pltpu.VMEM((tokens, width), BF16),
            pltpu.VMEM((heads, tokens), F32),
            pltpu.VMEM((heads, 3 * width), BF16),
            pltpu.SemaphoreType.DMA((5,)),
        ],
        compiler_params=params(LARGE),
        name="gate",
    )(q, k, v, decay_bias[0], gate)

    def chain(own, first, count, pairs):
        arrived = lax.ppermute(own, "seq", pairs)
        for _ in range(seq_size - 2):
            factor = kept * jnp.exp(cum[first : first + count, -1])[:, None, None]
            passed = factor * arrived.astype(F32) + own.astype(F32)
            arrived = lax.ppermute(passed.astype(BF16), "seq", pairs)
        return arrived

    entering = [chain(own, *group, forward) for own, group in zip(updates, groups)]
    outs, d_mixes, rows, grads = [], [], [], []
    for (first, count), state in zip(groups, entering):
        out_g, d_g, pushed, rows_g = pl.pallas_call(
            functools.partial(mix_kernel, first, count),
            out_shape=(
                shape((tokens, count * size), BF16),
                shape((tokens, count * size), BF16),
                shape((count, size, size), BF16),
                shape((count, tokens), F32),
            ),
            in_specs=[spec()] * 6 + [smem()],
            out_specs=(spec(),) * 4,
            compiler_params=params(),
            cost_estimate=cost(),
            name="mix",
        )(q, k, v, cot, cum, state, resets)
        outs.append(out_g)
        d_mixes.append(d_g)
        rows.append(rows_g)
        grads.append(chain(pushed, first, count, backward))

    output, gq, gk, gv, terms = pl.pallas_call(
        functools.partial(back_kernel, heads, groups),
        out_shape=(shape((tokens, width), BF16),)
        + (shape((tokens, width), F32),) * 3
        + (shape((heads, tokens), F32),),
        in_specs=[spec()] * 4 + [smem()] + [spec()] * (4 * len(groups)),
        out_specs=(spec(),) * 5,
        compiler_params=params(),
        cost_estimate=cost(),
        name="back",
    )(q, k, v, cum, resets, *outs, *d_mixes, *entering, *rows)
    if seq_size > 2:
        through = [
            kept * jnp.sum(g.astype(F32) * s.astype(F32), axis=(1, 2))[:, None]
            for g, s in zip(grads, entering)
        ]
        through = jnp.concatenate(through, axis=0)
    else:
        through = jnp.zeros((heads, 1), F32)

    share = 3 * width // dp_size
    halving = (
        dp_size > 1 and dp_size & (dp_size - 1) == 0 and share % 128 == 0 and seq_size == 2
    )
    order = [1 << b for b in range(dp_size.bit_length() - 1)] if halving else None
    if halving:
        part_shapes = (shape((dp_size // 2, heads, share), BF16),) * 2
    else:
        part_shapes = (shape((heads, 3 * width), F32),)
    place = lax.axis_index("dp").astype(jnp.int32).reshape(1)
    d_logits, *parts = pl.pallas_call(
        functools.partial(logit_kernel, heads, groups, order),
        out_shape=(shape((heads, tokens), BF16),) + part_shapes,
        in_specs=[spec()] * 7 + [smem()] + [spec()] * len(groups),
        out_specs=(spec(),) * (1 + len(part_shapes)),
        compiler_params=params(),
        cost_estimate=cost(),
        name="logits",
    )(q, k, v, cum, logits, terms, through, place, *grads)

    def finish(kernel, *arrays):
        return pl.pallas_call(
            kernel,
            out_shape=shape((tokens, width), BF16),
            in_specs=[spec()] * len(arrays),
            out_specs=spec(),
            compiler_params=params(),
            cost_estimate=cost(),
            name="finish",
        )(*arrays)

    grad_q = finish(finish_q_kernel, gq, d_logits, gate)
    grad_k = finish(
        functools.partial(finish_k_kernel, groups), gk, v, cum, d_logits, gate, *grads
    )
    grad_v = finish(
        functools.partial(finish_v_kernel, groups), gv, k, cum, d_logits, gate, *grads
    )

    if halving:
        keep, send = parts
        for step, mask in enumerate(order):
            arrived = lax.ppermute(send, "dp", [(i, i ^ mask) for i in range(dp_size)])
            total = keep.astype(F32) + arrived.astype(F32)
            half = total.shape[0] // 2
            if half:
                keep, send = total[:half].astype(BF16), total[half:].astype(BF16)
            if step == 0:
                send, grad_q = lax.optimization_barrier((send, grad_q))
            elif step == 1:
                send, grad_k = lax.optimization_barrier((send, grad_k))
            elif step == 2:
                send, grad_v = lax.optimization_barrier((send, grad_v))
        total = total[0]
        arrived = lax.ppermute(total.astype(BF16), "seq", [(0, 1), (1, 0)])
        total = total + arrived.astype(F32)
        piece = share // seq_size
        grad_gate = lax.dynamic_slice_in_dim(total, lax.axis_index("seq") * piece, piece, axis=1).T
    else:
        grad_gate = lax.psum_scatter(
            parts[0].T, ("dp", "seq"), scatter_dimension=0, tiled=True
        )
    return output[None], grad_q[None], grad_k[None], grad_v[None], grad_gate


def solution(mesh):
    rows = P("dp", "seq", None)
    return jax.shard_map(
        functools.partial(body, mesh.shape["dp"], mesh.shape["seq"]),
        mesh=mesh,
        in_specs=(rows, rows, rows, P("dp", None, "seq"), P(), P("dp", "seq"), rows),
        out_specs=(rows, rows, rows, rows, P(("dp", "seq"), None)),
        check_vma=False,
    )
```

```python
import functools

import jax
import jax.numpy as jnp
from jax import lax
from jax.experimental import pallas as pl
from jax.experimental.pallas import tpu as pltpu
from jax.sharding import PartitionSpec as P

EPSILON = 1e-06
F32 = jnp.float32
BF16 = jnp.bfloat16
STAGE = 8
VMEM_LIMIT = 16 * 1024 * 1024
VMEM_FULL = 51 * 1024 * 1024


def dot_nn(a, b):
    return lax.dot_general(a, b, (((1,), (0,)), ((), ())), preferred_element_type=F32)


def dot_nt(a, b):
    return lax.dot_general(a, b, (((1,), (1,)), ((), ())), preferred_element_type=F32)


def dot_tn(a, b):
    return lax.dot_general(a, b, (((0,), (0,)), ((), ())), preferred_element_type=F32)


def exact_dot(x, ones):
    rows = x.shape[0]
    high = x.astype(BF16)
    rest = x - high.astype(F32)
    middle = rest.astype(BF16)
    low = (rest - middle.astype(F32)).astype(BF16)
    parts = dot_nn(jnp.concatenate([high, middle, low], axis=0), ones)
    return parts[:rows] + parts[rows : 2 * rows] + parts[2 * rows :]


def triangle(size, upper):
    rows = lax.broadcasted_iota(jnp.int32, (size, size), 0)
    columns = lax.broadcasted_iota(jnp.int32, (size, size), 1)
    keep = rows <= columns if upper else rows >= columns
    return jnp.where(keep, 1.0, 0.0).astype(BF16)


def decay_matrix(cum_column, cum_row):
    size = cum_row.shape[1]
    rows = lax.broadcasted_iota(jnp.int32, (size, size), 0)
    columns = lax.broadcasted_iota(jnp.int32, (size, size), 1)
    return jnp.exp(jnp.where(columns <= rows, cum_column - cum_row, -jnp.inf))


def spec():
    return pl.BlockSpec(memory_space=pltpu.VMEM)


def smem():
    return pl.BlockSpec(memory_space=pltpu.SMEM)


def hbm():
    return pl.BlockSpec(memory_space=pltpu.HBM)


def params(limit=VMEM_LIMIT):
    return pltpu.CompilerParams(vmem_limit_bytes=limit)


def cost():
    return pl.CostEstimate(flops=1000, bytes_accessed=1000, transcendentals=0)


def head_lanes(size, first, count):
    return [slice(h * size, (h + 1) * size) for h in range(first, first + count)]


def add_updates(k, v, cum, groups, outs):
    size = outs[0].shape[1]
    fading = jnp.exp(cum[:, cum.shape[1] - 1 :] - cum)
    for (first, count), out in zip(groups, outs):
        parts = head_lanes(size, first, count)
        turned = [k[:, p].astype(F32).T for p in parts]
        faded = [(t * fading[first + i : first + i + 1, :]).astype(BF16) for i, t in enumerate(turned)]
        products = [dot_nn(f, v[:, p]) for f, p in zip(faded, parts)]
        for i, product in enumerate(products):
            out[i] = product.astype(BF16)


def gate_kernel(groups, q_in, k_in, v_in, cot_in, bias_in, gate_in, resets, *refs):
    logits_ref, cum_ref, rise_ref, *updates = refs[: 3 + len(groups)]
    q, k, v, cot, bias, gate, sems = refs[3 + len(groups) :]
    pairs = ((gate_in, gate), (bias_in, bias), (k_in, k), (q_in, q), (v_in, v), (cot_in, cot))
    copies = [
        pltpu.make_async_copy(source, target, sems.at[i])
        for i, (source, target) in enumerate(pairs)
    ]
    for copy in copies[:5]:
        copy.start()
    width = q.shape[1]
    for copy in copies[:3]:
        copy.wait()
    logits = bias[...] + dot_nt(gate[:, width : 2 * width], k[...])
    copies[3].wait()
    logits = logits + dot_nt(gate[:, :width], q[...])
    copies[4].wait()
    copies[5].start()
    logits = logits + dot_nt(gate[:, 2 * width :], v[...])
    logits_ref[...] = logits
    soft = jnp.maximum(logits, 0.0) + jnp.log1p(jnp.exp(-jnp.abs(logits)))
    cum = exact_dot(-soft, triangle(logits.shape[1], True))
    cum_ref[...] = cum
    rise_ref[...] = (1 - resets[0, 0]).astype(F32) * jnp.exp(cum)
    add_updates(k, v, cum, groups, updates)
    copies[5].wait()


def within_kernel(heads, q, k, v, cum_ref, attn_ref, within):
    size = q.shape[1] // heads
    cum_columns = cum_ref[...].T
    step = min(heads, STAGE)
    for first in range(0, heads, step):
        count = min(step, heads - first)
        parts = head_lanes(size, first, count)
        scores = [dot_nt(q[:, p], k[:, p]) for p in parts]
        attns = [
            (decay_matrix(cum_columns[:, h : h + 1], cum_ref[h : h + 1, :]) * s).astype(BF16)
            for h, s in enumerate(scores, first)
        ]
        for h, a in enumerate(attns, first):
            attn_ref[h] = a
        for a, p in zip(attns, parts):
            within[:, p] = dot_nn(a, v[:, p])


def mix_kernel(first, count, q, within, cot, rise_ref, state, *refs):
    *forwarded, out, d_mix, pushed, row_ref = refs
    size = state.shape[1]
    opening = lax.axis_index("seq") == 0
    parts, owns = head_lanes(size, first, count), head_lanes(size, 0, count)
    rise = rise_ref[...][first : first + count]
    decays = jnp.where(opening, 0.0, rise).T
    reads = [dot_nn(q[:, p], state[i]) for i, p in enumerate(parts)]
    mixtures = [
        within[:, p] + decays[:, i : i + 1] * x for i, (p, x) in enumerate(zip(parts, reads))
    ]
    upstream = [cot[:, p].astype(F32) for p in parts]
    squares = [jnp.mean(m * m, axis=1, keepdims=True) + EPSILON for m in mixtures]
    shared = [jnp.mean(u * m, axis=1, keepdims=True) for u, m in zip(upstream, mixtures)]
    inverses = [lax.rsqrt(s) for s in squares]
    normed = [m * i for m, i in zip(mixtures, inverses)]
    for n, o in zip(normed, owns):
        out[:, o] = n.astype(BF16)
    grads = [
        ((u - n * (s * i)) * i).astype(BF16)
        for u, n, s, i in zip(upstream, normed, shared, inverses)
    ]
    for g, o in zip(grads, owns):
        d_mix[:, o] = g
    faded = [
        (q[:, p].astype(F32).T * rise[i : i + 1, :]).astype(BF16) for i, p in enumerate(parts)
    ]
    products = [dot_nn(f, g) for f, g in zip(faded, grads)]
    for i, product in enumerate(products):
        product = product.astype(BF16)
        if forwarded:
            product = jnp.where(opening, forwarded[0][i], product)
        pushed[i] = product
    terms = [
        jnp.sum(g.astype(F32) * m, axis=1, keepdims=True) for g, m in zip(grads, mixtures)
    ]
    row_ref[...] = jnp.concatenate(terms, axis=1).T


def members(groups):
    return [(g, i) for g, (_, count) in enumerate(groups) for i in range(count)]


def back_kernel(groups, *refs):
    q, k, v, attn, cum_ref, rise_ref = refs[:6]
    number = len(groups)
    outs, d_mixes, states, row_terms = [refs[6 + number * i : 6 + number * (i + 1)] for i in range(4)]
    output, gq, gk, gv, term_ref, sems = refs[6 + 4 * number :]
    size = states[0].shape[1]
    copies = [
        pltpu.make_async_copy(
            out, output.at[:, pl.ds(first * size, count * size)], sems.at[i]
        )
        for i, ((first, count), out) in enumerate(zip(groups, outs))
    ]
    for copy in copies:
        copy.start()
    cum_columns = cum_ref[...].T
    rise_columns = jnp.where(lax.axis_index("seq") == 0, 0.0, rise_ref[...]).T
    sums = []
    places = members(groups)
    for start in range(0, len(places), STAGE):
        some = places[start : start + STAGE]
        heads = range(start, start + len(some))
        parts = head_lanes(size, start, len(some))
        grads = [d_mixes[g][:, i * size : (i + 1) * size] for g, i in some]
        columns = [cum_columns[:, h : h + 1] for h in heads]
        d_attns = [dot_nt(d, v[:, p]) for d, p in zip(grads, parts)]
        reads = [dot_nt(d, states[g][i]) for d, (g, i) in zip(grads, some)]
        weighted = [
            (decay_matrix(c, cum_ref[h : h + 1, :]) * d).astype(BF16)
            for h, c, d in zip(heads, columns, d_attns)
        ]
        for h, p, w, x in zip(heads, parts, weighted, reads):
            gq[:, p] = dot_nn(w, k[:, p]) + rise_columns[:, h : h + 1] * x
        for p, w in zip(parts, weighted):
            gk[:, p] = dot_tn(w, q[:, p])
        for h, p, d in zip(heads, parts, grads):
            gv[:, p] = dot_tn(attn[h], d)
        for h, d in zip(heads, d_attns):
            sums.append(jnp.sum(attn[h].astype(F32) * d, axis=0, keepdims=True))
    term_ref[...] = jnp.concatenate([r[...] for r in row_terms], axis=0) - jnp.concatenate(
        sums, axis=0
    )
    for copy in copies:
        copy.wait()


def logit_kernel(groups, order, slots, q, k, v, cum_ref, logits_ref, terms, through, *refs):
    grads = refs[: len(groups)]
    d_ref, *outs = refs[len(groups) :]
    size = grads[0].shape[1]
    width = q.shape[1]
    cum = cum_ref[...]
    tokens = cum.shape[1]
    totals = cum[:, tokens - 1 :]
    parts = head_lanes(size, 0, cum.shape[0])
    moved = [dot_nt(v[:, p], grads[g][i]) for p, (g, i) in zip(parts, members(groups))]
    sums = [jnp.sum(k[:, p].astype(F32) * m, axis=1, keepdims=True) for p, m in zip(parts, moved)]
    closing = lax.axis_index("seq") == slots - 1
    from_state = jnp.concatenate(sums, axis=1).T * jnp.where(closing, 0.0, jnp.exp(totals - cum))
    ends = jnp.sum(from_state, axis=1, keepdims=True) + jnp.exp(totals) * through[...]
    last = lax.broadcasted_iota(jnp.int32, cum.shape, 1) == tokens - 1
    d_cum = terms[...] - from_state + jnp.where(last, ends, 0.0)
    d_decay = exact_dot(d_cum, triangle(tokens, False))
    d_logits = (-jax.nn.sigmoid(logits_ref[...]) * d_decay).astype(BF16)
    d_ref[...] = d_logits
    whole = [dot_nn(d_logits, x[...]) for x in (q, k, v)]
    if order is None:
        for i in range(3):
            outs[0][:, i * width : (i + 1) * width] = whole[i]
        return
    keep, send, pieces = outs
    chunks, _, share = pieces.shape
    joined = jnp.concatenate([w.astype(BF16) for w in whole], axis=1)
    for j in range(chunks):
        pieces[j] = joined[:, j * share : (j + 1) * share]
    mine = lax.axis_index("dp")
    half = chunks // 2
    for position in range(chunks):
        relative = sum(mask for bit, mask in enumerate(order) if position & (chunks >> (bit + 1)))
        piece = pieces[mine ^ relative]
        if position < half:
            keep[position] = piece
        else:
            send[position - half] = piece


def finish_kernel(groups, index, rows, slots, partial, d_logits, gate, *refs):
    *refs, out, result, sems = refs
    width = partial.shape[1]
    places = members(groups)
    size = width // len(places)
    if rows is not None:
        operand, cum_ref, *grads = refs
        cum = cum_ref[...]
        closing = lax.axis_index("seq") == slots - 1
        fading = jnp.where(closing, 0.0, jnp.exp(cum[:, cum.shape[1] - 1 :] - cum)).T
    copies = []
    for start in range(0, len(places), STAGE):
        some = places[start : start + STAGE]
        lanes = slice(start * size, (start + len(some)) * size)
        at = index * width + start * size
        back = dot_tn(d_logits[...], gate[:, at : at + len(some) * size])
        if rows is None:
            result[:, lanes] = (partial[:, lanes] + back).astype(BF16)
        else:
            parts, owns = head_lanes(size, start, len(some)), head_lanes(size, 0, len(some))
            moved = [rows(operand[:, p], grads[g][i]) for p, (g, i) in zip(parts, some)]
            for i, (p, o, m) in enumerate(zip(parts, owns, moved)):
                h = start + i
                total = partial[:, p] + fading[:, h : h + 1] * m + back[:, o]
                result[:, p] = total.astype(BF16)
        at = pl.ds(start * size, len(some) * size)
        copies.append(
            pltpu.make_async_copy(result.at[:, at], out.at[:, at], sems.at[start // STAGE])
        )
        copies[-1].start()
    for copy in copies:
        copy.wait()


def shape(dims, dtype):
    return jax.ShapeDtypeStruct(dims, dtype)


def head_groups(heads):
    parts = 4 if heads >= 4 else 1
    sizes = [heads // parts + (1 if i < heads % parts else 0) for i in range(parts)]
    return [(sum(sizes[:i]), sizes[i]) for i in range(parts)]


def body(dp_size, seq_size, queries, keys, values, decay_bias, gate_matrix, resets, cotangent):
    q, k, v, cot = queries[0], keys[0], values[0], cotangent[0]
    tokens, width = q.shape
    heads = decay_bias.shape[1]
    size = width // heads
    gate = gate_matrix.T
    groups = head_groups(heads)
    forward = [(i, i + 1) for i in range(seq_size - 1)]
    backward = [(i + 1, i) for i in range(seq_size - 1)]
    slot = lax.axis_index("seq")
    kept = (1 - resets[0, 0]).astype(F32)

    def state_shapes(some):
        return tuple(shape((count, size, size), BF16) for _, count in some)

    logits, cum, rise, *made = pl.pallas_call(
        functools.partial(gate_kernel, groups),
        out_shape=(shape((heads, tokens), F32),) * 3
        + state_shapes(groups)
        + (shape((tokens, width), BF16),) * 4,
        in_specs=[hbm()] * 6 + [smem()],
        out_specs=(spec(),) * (7 + len(groups)),
        scratch_shapes=[
            pltpu.VMEM((heads, tokens), F32),
            pltpu.VMEM((heads, 3 * width), BF16),
            pltpu.SemaphoreType.DMA((6,)),
        ],
        compiler_params=params(VMEM_FULL),
        cost_estimate=cost(),
        name="gate",
    )(q, k, v, cot, decay_bias[0], gate, resets)
    *updates, q, k, v, cot = made

    def chain(own, first, count, pairs):
        if seq_size == 2:
            return lax.ppermute(own, "seq", [(0, 1), (1, 0)])
        arrived = lax.ppermute(own, "seq", pairs)
        for _ in range(seq_size - 2):
            factor = kept * jnp.exp(cum[first : first + count, -1])[:, None, None]
            passed = factor * arrived.astype(F32) + own.astype(F32)
            arrived = lax.ppermute(passed.astype(BF16), "seq", pairs)
        return arrived

    ahead = 2 if seq_size == 2 and len(groups) == 4 else len(groups)
    entering = [chain(updates[g], *groups[g], forward) for g in range(min(ahead, len(groups)))]
    attn, within = pl.pallas_call(
        functools.partial(within_kernel, heads),
        out_shape=(shape((heads, tokens, tokens), BF16), shape((tokens, width), F32)),
        in_specs=[spec()] * 4,
        out_specs=(spec(),) * 2,
        compiler_params=params(),
        cost_estimate=cost(),
        name="within",
    )(q, k, v, cum)
    outs, d_mixes, rows, grads = [], [], [], []
    for g, (first, count) in enumerate(groups):
        forwarded = [updates[g + ahead]] if g + ahead < len(groups) else []
        out_g, d_g, pushed, rows_g = pl.pallas_call(
            functools.partial(mix_kernel, first, count),
            out_shape=(
                shape((tokens, count * size), BF16),
                shape((tokens, count * size), BF16),
                shape((count, size, size), BF16),
                shape((count, tokens), F32),
            ),
            in_specs=[spec()] * (5 + len(forwarded)),
            out_specs=(spec(),) * 4,
            compiler_params=params(),
            cost_estimate=cost(),
            name="mix",
        )(q, within, cot, rise, entering[g], *forwarded)
        outs.append(out_g)
        d_mixes.append(d_g)
        rows.append(rows_g)
        if forwarded:
            arrived = lax.ppermute(pushed, "seq", [(0, 1), (1, 0)])
            entering.append(arrived)
            grads.append(arrived)
        else:
            grads.append(chain(pushed, first, count, backward))

    output, gq, gk, gv, terms = pl.pallas_call(
        functools.partial(back_kernel, groups),
        out_shape=(shape((tokens, width), BF16),)
        + (shape((tokens, width), F32),) * 3
        + (shape((heads, tokens), F32),),
        in_specs=[spec()] * (6 + 4 * len(groups)),
        out_specs=(hbm(),) + (spec(),) * 4,
        scratch_shapes=[pltpu.SemaphoreType.DMA((len(groups),))],
        compiler_params=params(),
        cost_estimate=cost(),
        name="back",
    )(q, k, v, attn, cum, rise, *outs, *d_mixes, *entering, *rows)
    if seq_size > 2:
        through = [
            kept * jnp.sum(g.astype(F32) * s.astype(F32), axis=(1, 2))[:, None]
            for g, s in zip(grads, entering)
        ]
        through = jnp.concatenate(through, axis=0)
    else:
        through = jnp.zeros((heads, 1), F32)

    share = 3 * width // dp_size
    halving = (
        dp_size > 1 and dp_size & (dp_size - 1) == 0 and share % 128 == 0 and seq_size == 2
    )
    order = [1 << b for b in range(dp_size.bit_length() - 1)] if halving else None
    if halving:
        part_shapes = (shape((dp_size // 2, heads, share), BF16),) * 2
        scratch = [pltpu.VMEM((dp_size, heads, share), BF16)]
    else:
        part_shapes = (shape((heads, 3 * width), F32),)
        scratch = []
    d_logits, *parts = pl.pallas_call(
        functools.partial(logit_kernel, groups, order, seq_size),
        out_shape=(shape((heads, tokens), BF16),) + part_shapes,
        in_specs=[spec()] * (7 + len(groups)),
        out_specs=(spec(),) * (1 + len(part_shapes)),
        scratch_shapes=scratch,
        compiler_params=params(),
        cost_estimate=cost(),
        name="logits",
    )(q, k, v, cum, logits, terms, through, *grads)

    def finish(index, rows, partial, *extra):
        return pl.pallas_call(
            functools.partial(finish_kernel, groups, index, rows, seq_size),
            out_shape=shape((tokens, width), BF16),
            in_specs=[spec()] * (3 + len(extra)),
            out_specs=hbm(),
            scratch_shapes=[
                pltpu.VMEM((tokens, width), BF16),
                pltpu.SemaphoreType.DMA((-(-heads // STAGE),)),
            ],
            compiler_params=params(),
            cost_estimate=cost(),
            name="finish",
        )(partial, d_logits, gate, *extra)

    grad_q = finish(0, None, gq)
    grad_k = finish(1, dot_nt, gk, v, cum, *grads)
    grad_v = finish(2, dot_nn, gv, k, cum, *grads)

    if halving:
        keep, send = parts
        for step, mask in enumerate(order):
            arrived = lax.ppermute(send, "dp", [(i, i ^ mask) for i in range(dp_size)])
            total = keep.astype(F32) + arrived.astype(F32)
            half = total.shape[0] // 2
            if half:
                keep, send = total[:half].astype(BF16), total[half:].astype(BF16)
            if step == 1:
                send, grad_q = lax.optimization_barrier((send, grad_q))
            elif step == 2:
                send, grad_k = lax.optimization_barrier((send, grad_k))
            elif step == 3:
                total, grad_v = lax.optimization_barrier((total, grad_v))
        total = total[0]
        arrived = lax.ppermute(total.astype(BF16), "seq", [(0, 1), (1, 0)])
        total = total + arrived.astype(F32)
        piece = share // seq_size
        grad_gate = lax.dynamic_slice_in_dim(total, slot * piece, piece, axis=1).T
    else:
        grad_gate = lax.psum_scatter(
            parts[0].T, ("dp", "seq"), scatter_dimension=0, tiled=True
        )
    return output[None], grad_q[None], grad_k[None], grad_v[None], grad_gate


def solution(mesh):
    rows = P("dp", "seq", None)
    return jax.shard_map(
        functools.partial(body, mesh.shape["dp"], mesh.shape["seq"]),
        mesh=mesh,
        in_specs=(rows, rows, rows, P("dp", None, "seq"), P(), P("dp", "seq"), rows),
        out_specs=(rows, rows, rows, rows, P(("dp", "seq"), None)),
        check_vma=False,
    )
```

```python
import functools

import jax
import jax.numpy as jnp
from jax import lax
from jax.experimental import pallas as pl
from jax.experimental.pallas import tpu as pltpu
from jax.sharding import PartitionSpec as P

EPSILON = 1e-06
F32 = jnp.float32
BF16 = jnp.bfloat16
STAGE = 8
CORES = 2
VMEM_LIMIT = 16 * 1024 * 1024
VMEM_FULL = 58 * 1024 * 1024


def dot_nn(a, b):
    return lax.dot_general(a, b, (((1,), (0,)), ((), ())), preferred_element_type=F32)


def dot_nt(a, b):
    return lax.dot_general(a, b, (((1,), (1,)), ((), ())), preferred_element_type=F32)


def dot_tn(a, b):
    return lax.dot_general(a, b, (((0,), (0,)), ((), ())), preferred_element_type=F32)


def exact_dot(x, ones):
    rows = x.shape[0]
    high = x.astype(BF16)
    rest = x - high.astype(F32)
    middle = rest.astype(BF16)
    low = (rest - middle.astype(F32)).astype(BF16)
    parts = dot_nn(jnp.concatenate([high, middle, low], axis=0), ones)
    return parts[:rows] + parts[rows : 2 * rows] + parts[2 * rows :]


def triangle(size, upper):
    rows = lax.broadcasted_iota(jnp.int32, (size, size), 0)
    columns = lax.broadcasted_iota(jnp.int32, (size, size), 1)
    keep = rows <= columns if upper else rows >= columns
    return jnp.where(keep, 1.0, 0.0).astype(BF16)


def decay_matrix(cum_column, cum_row):
    size = cum_row.shape[1]
    rows = lax.broadcasted_iota(jnp.int32, (size, size), 0)
    columns = lax.broadcasted_iota(jnp.int32, (size, size), 1)
    return jnp.exp(jnp.where(columns <= rows, cum_column - cum_row, -jnp.inf))


def spec():
    return pl.BlockSpec(memory_space=pltpu.VMEM)


def smem():
    return pl.BlockSpec(memory_space=pltpu.SMEM)


def hbm():
    return pl.BlockSpec(memory_space=pltpu.HBM)


def params(limit=VMEM_LIMIT):
    return pltpu.CompilerParams(vmem_limit_bytes=limit)


def cost():
    return pl.CostEstimate(flops=1000, bytes_accessed=1000, transcendentals=0)


def head_lanes(size, first, count):
    return [slice(h * size, (h + 1) * size) for h in range(first, first + count)]


def turn(k, size, groups):
    return [
        [k[:, p].astype(F32).T for p in head_lanes(size, first, count)] for first, count in groups
    ]


def add_updates(turned, v, cum, groups, outs):
    size = outs[0].shape[1]
    fading = jnp.exp(cum[:, cum.shape[1] - 1 :] - cum)
    faded = [
        [(t * fading[first + i : first + i + 1, :]).astype(BF16) for i, t in enumerate(some)]
        for (first, _), some in zip(groups, turned)
    ]
    for (first, count), some, out in zip(groups, faded, outs):
        parts = head_lanes(size, first, count)
        for i, product in enumerate([dot_nn(f, v[:, p]) for f, p in zip(some, parts)]):
            out[i] = product.astype(BF16)


def gate_kernel(groups, q_in, k_in, v_in, bias_in, gate_in, *refs):
    logits_ref, cum_ref, *updates = refs[: 2 + len(groups)]
    q, k, v, bias, gate, sems = refs[2 + len(groups) :]
    pairs = ((gate_in, gate), (bias_in, bias), (k_in, k), (q_in, q), (v_in, v))
    copies = [
        pltpu.make_async_copy(source, target, sems.at[i])
        for i, (source, target) in enumerate(pairs)
    ]
    for copy in copies:
        copy.start()
    width = q.shape[1]
    for copy in copies[:3]:
        copy.wait()
    logits = bias[...] + dot_nt(gate[:, width : 2 * width], k[...])
    turned = turn(k, updates[0].shape[1], groups)
    copies[3].wait()
    logits = logits + dot_nt(gate[:, :width], q[...])
    copies[4].wait()
    logits = logits + dot_nt(gate[:, 2 * width :], v[...])
    logits_ref[...] = logits
    soft = jnp.maximum(logits, 0.0) + jnp.log1p(jnp.exp(-jnp.abs(logits)))
    cum = exact_dot(-soft, triangle(logits.shape[1], True))
    cum_ref[...] = cum
    add_updates(turned, v, cum, groups, updates)


def within_kernel(heads, groups, q, k, v, cum_ref, cot, resets, attn_ref, within, rise_ref, *updates):
    del cot
    rise_ref[...] = (1 - resets[0, 0]).astype(F32) * jnp.exp(cum_ref[...])
    size = q.shape[1] // heads
    if groups:
        add_updates(turn(k, size, groups), v, cum_ref[...], groups, updates)
    cum_columns = cum_ref[...].T
    step = min(heads, STAGE)
    for first in range(0, heads, step):
        count = min(step, heads - first)
        parts = head_lanes(size, first, count)
        scores = [dot_nt(q[:, p], k[:, p]) for p in parts]
        attns = [
            (decay_matrix(cum_columns[:, h : h + 1], cum_ref[h : h + 1, :]) * s).astype(BF16)
            for h, s in enumerate(scores, first)
        ]
        for h, a in enumerate(attns, first):
            attn_ref[h] = a
        for a, p in zip(attns, parts):
            within[:, p] = dot_nn(a, v[:, p])


def mix_kernel(first, count, q, within, cot, rise_ref, state, *refs):
    *forwarded, out, d_mix, pushed, row_ref = refs
    size = state.shape[1]
    opening = lax.axis_index("seq") == 0
    parts, owns = head_lanes(size, first, count), head_lanes(size, 0, count)
    rise = rise_ref[...][first : first + count]
    decays = jnp.where(opening, 0.0, rise).T
    reads = [dot_nn(q[:, p], state[i]) for i, p in enumerate(parts)]
    mixtures = [
        within[:, p] + decays[:, i : i + 1] * x for i, (p, x) in enumerate(zip(parts, reads))
    ]
    upstream = [cot[:, p].astype(F32) for p in parts]
    squares = [jnp.mean(m * m, axis=1, keepdims=True) + EPSILON for m in mixtures]
    shared = [jnp.mean(u * m, axis=1, keepdims=True) for u, m in zip(upstream, mixtures)]
    inverses = [lax.rsqrt(s) for s in squares]
    normed = [m * i for m, i in zip(mixtures, inverses)]
    for n, o in zip(normed, owns):
        out[:, o] = n.astype(BF16)
    grads = [
        ((u - n * (s * i)) * i).astype(BF16)
        for u, n, s, i in zip(upstream, normed, shared, inverses)
    ]
    for g, o in zip(grads, owns):
        d_mix[:, o] = g
    faded = [
        (q[:, p].astype(F32).T * rise[i : i + 1, :]).astype(BF16) for i, p in enumerate(parts)
    ]
    products = [dot_nn(f, g) for f, g in zip(faded, grads)]
    for i, product in enumerate(products):
        product = product.astype(BF16)
        if forwarded:
            product = jnp.where(opening, forwarded[0][i], product)
        pushed[i] = product
    terms = [
        jnp.sum(g.astype(F32) * m, axis=1, keepdims=True) for g, m in zip(grads, mixtures)
    ]
    row_ref[...] = jnp.concatenate(terms, axis=1).T


def members(groups):
    return [(g, i) for g, (_, count) in enumerate(groups) for i in range(count)]


def fading_rows(cum, slots):
    closing = lax.axis_index("seq") == slots - 1
    return jnp.where(closing, 0.0, jnp.exp(cum[:, cum.shape[1] - 1 :] - cum))


def state_terms(keys, moved, fading):
    sums = [jnp.sum(x.astype(F32) * m, axis=1, keepdims=True) for x, m in zip(keys, moved)]
    from_state = jnp.concatenate(sums, axis=1).T * fading
    last = lax.broadcasted_iota(jnp.int32, fading.shape, 1) == fading.shape[1] - 1
    total = jnp.sum(from_state, axis=1, keepdims=True)
    return jnp.where(last, total, 0.0) - from_state


def back_kernel(groups, early, slots, *refs):
    q, k, v, attn, cum_ref, rise_ref = refs[:6]
    number = len(groups)
    outs, d_mixes, states, row_terms = [refs[6 + number * i : 6 + number * (i + 1)] for i in range(4)]
    *grads, output, gq, gk, gv, term_ref, sems = refs[6 + 4 * number :]
    size = states[0].shape[1]
    copies = [
        pltpu.make_async_copy(
            out, output.at[:, pl.ds(first * size, count * size)], sems.at[i]
        )
        for i, ((first, count), out) in enumerate(zip(groups, outs))
    ]
    for copy in copies:
        copy.start()
    cum = cum_ref[...]
    cum_columns = cum.T
    rise_columns = jnp.where(lax.axis_index("seq") == 0, 0.0, rise_ref[...]).T
    fading = fading_rows(cum, slots)
    fading_columns = fading.T
    sums, added = [], []
    places = members(groups)
    for start in range(0, len(places), STAGE):
        some = places[start : start + STAGE]
        heads = range(start, start + len(some))
        parts = head_lanes(size, start, len(some))
        d_outs = [d_mixes[g][:, i * size : (i + 1) * size] for g, i in some]
        columns = [cum_columns[:, h : h + 1] for h in heads]
        d_attns = [dot_nt(d, v[:, p]) for d, p in zip(d_outs, parts)]
        reads = [dot_nt(d, states[g][i]) for d, (g, i) in zip(d_outs, some)]
        weighted = [
            (decay_matrix(c, cum_ref[h : h + 1, :]) * d).astype(BF16)
            for h, c, d in zip(heads, columns, d_attns)
        ]
        ready = [(h, p, g, i) for h, p, (g, i) in zip(heads, parts, some) if g < early]
        moved_k = {h: dot_nt(v[:, p], grads[g][i]) for h, p, g, i in ready}
        moved_v = {h: dot_nn(k[:, p], grads[g][i]) for h, p, g, i in ready}
        for h, p, w, x in zip(heads, parts, weighted, reads):
            gq[:, p] = dot_nn(w, k[:, p]) + rise_columns[:, h : h + 1] * x
        for h, p, w in zip(heads, parts, weighted):
            total = dot_tn(w, q[:, p])
            gk[:, p] = total + fading_columns[:, h : h + 1] * moved_k[h] if h in moved_k else total
        for h, p, d in zip(heads, parts, d_outs):
            total = dot_tn(attn[h], d)
            gv[:, p] = total + fading_columns[:, h : h + 1] * moved_v[h] if h in moved_v else total
        for h, d in zip(heads, d_attns):
            sums.append(jnp.sum(attn[h].astype(F32) * d, axis=0, keepdims=True))
        if ready:
            first = ready[0][0]
            keys = [k[:, p] for _, p, _, _ in ready]
            some_fading = fading[first : first + len(ready)]
            added.append(state_terms(keys, [moved_k[h] for h, *_ in ready], some_fading))
    terms = jnp.concatenate([r[...] for r in row_terms], axis=0) - jnp.concatenate(sums, axis=0)
    if added:
        early_terms = jnp.concatenate(added, axis=0)
        count = early_terms.shape[0]
        term_ref[:count, :] = terms[:count] + early_terms
        term_ref[count:, :] = terms[count:]
    else:
        term_ref[...] = terms
    for copy in copies:
        copy.wait()


def logit_kernel(groups, early, slots, q, k, v, cum_ref, logits_ref, terms, through, *refs):
    late = len(groups) - early
    grads, (d_ref, *outs) = refs[:late], refs[late:]
    size = grads[0].shape[1]
    width = q.shape[1]
    cum = cum_ref[...]
    tokens = cum.shape[1]
    first = groups[early][0]
    parts = head_lanes(size, first, cum.shape[0] - first)
    moved = [dot_nt(v[:, p], grads[g][i]) for p, (g, i) in zip(parts, members(groups[early:]))]
    added = state_terms([k[:, p] for p in parts], moved, fading_rows(cum, slots)[first:])
    d_cum = terms[...] + through[...]
    d_cum = jnp.concatenate([d_cum[:first], d_cum[first:] + added], axis=0) if first else d_cum + added
    d_decay = exact_dot(d_cum, triangle(tokens, False))
    d_logits = (-jax.nn.sigmoid(logits_ref[...]) * d_decay).astype(BF16)
    d_ref[...] = d_logits
    whole = [dot_nn(d_logits, x[...]) for x in (q, k, v)]
    if len(outs) == 1:
        for i in range(3):
            outs[0][:, i * width : (i + 1) * width] = whole[i]
        return
    keep, send, pieces = outs
    joined = jnp.concatenate(whole, axis=1)
    cores, others = pieces.shape[:2]
    piece = 3 * width // (cores * others)
    for j in range(others):
        for c in range(cores):
            row, slot = j // slots * cores + c, j % slots
            pieces[c, j] = pack(joined, (row * slots + slot) * piece, piece).astype(BF16)
    core = lax.axis_index("core")
    keep[...] = pieces[core]
    send[...] = pieces[1 - core]


def pack(joined, first, piece):
    tiles = [joined[:, first + i : first + i + 128] for i in range(0, piece - 127, 128)]
    if piece % 128:
        rest = joined[:, first + piece // 128 * 128 : first + piece]
        half = rest.shape[0] // 2
        tiles.append(jnp.concatenate([rest[:half], rest[half:]], axis=1))
    return jnp.concatenate(tiles, axis=0)


def sum_kernel(arrived, out):
    heads, piece = out.shape
    total = jnp.sum(arrived[...].astype(F32), axis=0)
    tiles = piece // 128
    for i in range(tiles):
        out[:, i * 128 : (i + 1) * 128] = total[i * heads : (i + 1) * heads]
    if piece % 128:
        rest = total[tiles * heads :]
        out[: heads // 2, tiles * 128 :] = rest[:, :64]
        out[heads // 2 :, tiles * 128 :] = rest[:, 64:]


def finish_kernel(groups, early, slots, gq, gk, gv, k, v, cum_ref, d_logits, gate, *refs):
    late = len(groups) - early
    grads, outs, (result, sems) = refs[:late], refs[late : late + 3], refs[late + 3 :]
    width = gq.shape[1]
    places = members(groups)
    size = width // len(places)
    fading = fading_rows(cum_ref[...], slots).T
    copies = []
    for index, (partial, operand) in enumerate(((gq, None), (gk, v), (gv, k))):
        for start in range(0, len(places), STAGE):
            some = places[start : start + STAGE]
            at = index * width + start * size
            back = dot_tn(d_logits[...], gate[:, at : at + len(some) * size])
            parts, owns = head_lanes(size, start, len(some)), head_lanes(size, 0, len(some))
            moved = {}
            for h, (p, (g, i)) in enumerate(zip(parts, some), start):
                if operand is not None and g >= early:
                    dot = dot_nt if index == 1 else dot_nn
                    moved[h] = dot(operand[:, p], grads[g - early][i])
            for h, (p, o) in enumerate(zip(parts, owns), start):
                total = partial[:, p] + back[:, o]
                if h in moved:
                    total = total + fading[:, h : h + 1] * moved[h]
                result[index, :, p] = total.astype(BF16)
            lanes = pl.ds(start * size, len(some) * size)
            copies.append(
                pltpu.make_async_copy(
                    result.at[index, :, lanes], outs[index].at[:, lanes], sems.at[len(copies)]
                )
            )
            copies[-1].start()
    for copy in copies:
        copy.wait()


def shape(dims, dtype):
    return jax.ShapeDtypeStruct(dims, dtype)


def head_groups(heads):
    parts = 4 if heads >= 4 else 1
    sizes = [heads // parts + (1 if i < heads % parts else 0) for i in range(parts)]
    return [(sum(sizes[:i]), sizes[i]) for i in range(parts)]


def body(
    pairs, cores, seq_size, queries, keys, values, decay_bias, gate_matrix, resets, cotangent
):
    q, k, v, cot = queries[0], keys[0], values[0], cotangent[0]
    tokens, width = q.shape
    heads = decay_bias.shape[1]
    size = width // heads
    gate = gate_matrix.T
    groups = head_groups(heads)
    forward = [(i, i + 1) for i in range(seq_size - 1)]
    backward = [(i + 1, i) for i in range(seq_size - 1)]
    kept = (1 - resets[0, 0]).astype(F32)

    def state_shapes(some):
        return tuple(shape((count, size, size), BF16) for _, count in some)

    ahead = 2 if seq_size == 2 and len(groups) > 2 else len(groups)
    logits, cum, *updates = pl.pallas_call(
        functools.partial(gate_kernel, groups[:ahead]),
        out_shape=(shape((heads, tokens), F32),) * 2
        + state_shapes(groups[:ahead]),
        in_specs=[hbm()] * 5,
        out_specs=(spec(),) * (2 + ahead),
        scratch_shapes=[
            pltpu.VMEM((tokens, width), BF16),
            pltpu.VMEM((tokens, width), BF16),
            pltpu.VMEM((tokens, width), BF16),
            pltpu.VMEM((heads, tokens), F32),
            pltpu.VMEM((heads, 3 * width), BF16),
            pltpu.SemaphoreType.DMA((5,)),
        ],
        compiler_params=params(VMEM_FULL),
        cost_estimate=cost(),
        name="gate",
    )(q, k, v, decay_bias[0], gate)
    attn, within, rise, *made = pl.pallas_call(
        functools.partial(within_kernel, heads, groups[ahead:]),
        out_shape=(
            shape((heads, tokens, tokens), BF16),
            shape((tokens, width), F32),
            shape((heads, tokens), F32),
        )
        + state_shapes(groups[ahead:]),
        in_specs=[spec()] * 5 + [smem()],
        out_specs=(spec(),) * (3 + len(groups) - ahead),
        compiler_params=params(),
        cost_estimate=cost(),
        name="within",
    )(q, k, v, cum, cot, resets)
    updates += made

    def chain(own, first, count, pairs):
        if seq_size == 2:
            return lax.ppermute(own, "seq", [(0, 1), (1, 0)])
        arrived = lax.ppermute(own, "seq", pairs)
        for _ in range(seq_size - 2):
            factor = kept * jnp.exp(cum[first : first + count, -1])[:, None, None]
            passed = factor * arrived.astype(F32) + own.astype(F32)
            arrived = lax.ppermute(passed.astype(BF16), "seq", pairs)
        return arrived

    entering = [chain(updates[g], *groups[g], forward) for g in range(ahead)]
    outs, d_mixes, rows, grads = [], [], [], []
    for g, (first, count) in enumerate(groups):
        forwarded = [updates[g + ahead]] if g + ahead < len(groups) else []
        out_g, d_g, pushed, rows_g = pl.pallas_call(
            functools.partial(mix_kernel, first, count),
            out_shape=(
                shape((tokens, count * size), BF16),
                shape((tokens, count * size), BF16),
                shape((count, size, size), BF16),
                shape((count, tokens), F32),
            ),
            in_specs=[spec()] * (5 + len(forwarded)),
            out_specs=(spec(),) * 4,
            compiler_params=params(),
            cost_estimate=cost(),
            name="mix",
        )(q, within, cot, rise, entering[g], *forwarded)
        outs.append(out_g)
        d_mixes.append(d_g)
        rows.append(rows_g)
        if forwarded:
            arrived = lax.ppermute(pushed, "seq", [(0, 1), (1, 0)])
            entering.append(arrived)
            grads.append(arrived)
        else:
            grads.append(chain(pushed, first, count, backward))

    early = min(ahead, len(groups) // 2)
    output, gq, gk, gv, terms = pl.pallas_call(
        functools.partial(back_kernel, groups, early, seq_size),
        out_shape=(shape((tokens, width), BF16),)
        + (shape((tokens, width), F32),) * 3
        + (shape((heads, tokens), F32),),
        in_specs=[spec()] * (6 + 4 * len(groups) + early),
        out_specs=(hbm(),) + (spec(),) * 4,
        scratch_shapes=[pltpu.SemaphoreType.DMA((len(groups),))],
        compiler_params=params(),
        cost_estimate=cost(),
        name="back",
    )(q, k, v, attn, cum, rise, *outs, *d_mixes, *entering, *rows, *grads[:early])
    if seq_size > 2:
        through = [
            kept * jnp.sum(g.astype(F32) * s.astype(F32), axis=(1, 2))[:, None]
            for g, s in zip(grads, entering)
        ]
        through = jnp.concatenate(through, axis=0) * jnp.exp(cum[:, -1:])
        through = through * (jnp.arange(tokens) == tokens - 1).astype(F32)
    else:
        through = jnp.zeros((heads, tokens), F32)

    piece = 3 * width // (pairs * CORES * seq_size)
    exchanged = cores == CORES and piece >= 128 and piece % 64 == 0 and heads % 16 == 0
    others = pairs * seq_size
    packed = piece * heads // 128
    if exchanged:
        part_shapes = (shape((others, packed, 128), BF16),) * 2
        scratch = [pltpu.VMEM((CORES, others, packed, 128), BF16)]
    else:
        part_shapes = (shape((heads, 3 * width), F32),)
        scratch = []
    d_logits, *parts = pl.pallas_call(
        functools.partial(logit_kernel, groups, early, seq_size),
        out_shape=(shape((heads, tokens), BF16),) + part_shapes,
        in_specs=[spec()] * (7 + len(groups) - early),
        out_specs=(spec(),) * (1 + len(part_shapes)),
        scratch_shapes=scratch,
        compiler_params=params(),
        cost_estimate=cost(),
        name="logits",
    )(q, k, v, cum, logits, terms, through, *grads[early:])

    input_grads = pl.pallas_call(
        functools.partial(finish_kernel, groups, early, seq_size),
        out_shape=(shape((tokens, width), BF16),) * 3,
        in_specs=[spec()] * (8 + len(groups) - early),
        out_specs=(hbm(),) * 3,
        scratch_shapes=[
            pltpu.VMEM((3, tokens, width), BF16),
            pltpu.SemaphoreType.DMA((3 * -(-heads // STAGE),)),
        ],
        compiler_params=params(),
        cost_estimate=cost(),
        name="finish",
    )(gq, gk, gv, k, v, cum, d_logits, gate, *grads[early:])

    if exchanged:
        keep, send = parts
        arrived = lax.ppermute(send, "core", [(0, 1), (1, 0)])
        total = (keep.astype(F32) + arrived.astype(F32)).astype(BF16)
        total, *input_grads = lax.optimization_barrier((total, *input_grads))
        arrived = lax.all_to_all(total, ("pair", "seq"), 0, 0, tiled=True)
        grad_gate = pl.pallas_call(
            sum_kernel,
            out_shape=shape((heads, piece), F32),
            in_specs=[spec()],
            out_specs=spec(),
            compiler_params=params(),
            name="sum",
        )(arrived).T
    else:
        grad_gate = lax.psum_scatter(
            parts[0].T, ("pair", "core", "seq"), scatter_dimension=0, tiled=True
        )
    return output[None], *[g[None] for g in input_grads], grad_gate


def solution(mesh):
    rows, slots = mesh.devices.shape
    cores = CORES if rows % CORES == 0 else 1
    devices = mesh.devices.reshape(rows // cores, cores, slots)
    mesh = jax.sharding.Mesh(devices, ("pair", "core", "seq"))
    row = ("pair", "core")
    tokens = P(row, "seq", None)
    return jax.shard_map(
        functools.partial(body, rows // cores, cores, slots),
        mesh=mesh,
        in_specs=(tokens, tokens, tokens, P(row, None, "seq"), P(), P(row, "seq"), tokens),
        out_specs=(tokens, tokens, tokens, tokens, P((*row, "seq"), None)),
        check_vma=False,
    )
```

```python
import functools

import jax
import jax.numpy as jnp
from jax import lax
from jax.experimental import pallas as pl
from jax.experimental.pallas import tpu as pltpu
from jax.sharding import PartitionSpec as P

EPSILON = 1e-06
F32 = jnp.float32
BF16 = jnp.bfloat16
STAGE = 8
CORES = 2
VMEM_LIMIT = 16 * 1024 * 1024
VMEM_FULL = 58 * 1024 * 1024


def dot_nn(a, b):
    return lax.dot_general(a, b, (((1,), (0,)), ((), ())), preferred_element_type=F32)


def dot_nt(a, b):
    return lax.dot_general(a, b, (((1,), (1,)), ((), ())), preferred_element_type=F32)


def dot_tn(a, b):
    return lax.dot_general(a, b, (((0,), (0,)), ((), ())), preferred_element_type=F32)


def exact_dot(x, ones):
    rows = x.shape[0]
    high = x.astype(BF16)
    rest = x - high.astype(F32)
    middle = rest.astype(BF16)
    low = (rest - middle.astype(F32)).astype(BF16)
    parts = dot_nn(jnp.concatenate([high, middle, low], axis=0), ones)
    return parts[:rows] + parts[rows : 2 * rows] + parts[2 * rows :]


def triangle(size, upper):
    rows = lax.broadcasted_iota(jnp.int32, (size, size), 0)
    columns = lax.broadcasted_iota(jnp.int32, (size, size), 1)
    keep = rows <= columns if upper else rows >= columns
    return jnp.where(keep, 1.0, 0.0).astype(BF16)


def decay_matrix(cum_column, cum_row):
    size = cum_row.shape[1]
    rows = lax.broadcasted_iota(jnp.int32, (size, size), 0)
    columns = lax.broadcasted_iota(jnp.int32, (size, size), 1)
    return jnp.exp(jnp.where(columns <= rows, cum_column - cum_row, -jnp.inf))


def spec():
    return pl.BlockSpec(memory_space=pltpu.VMEM)


def smem():
    return pl.BlockSpec(memory_space=pltpu.SMEM)


def hbm():
    return pl.BlockSpec(memory_space=pltpu.HBM)


def params(limit=VMEM_LIMIT):
    return pltpu.CompilerParams(vmem_limit_bytes=limit)


def cost():
    return pl.CostEstimate(flops=1000, bytes_accessed=1000, transcendentals=0)


def head_lanes(size, first, count):
    return [slice(h * size, (h + 1) * size) for h in range(first, first + count)]


def turn(k, size, groups):
    return [
        [k[:, p].astype(F32).T for p in head_lanes(size, first, count)] for first, count in groups
    ]


def add_updates(turned, v, cum, groups, outs):
    size = outs[0].shape[1]
    fading = jnp.exp(cum[:, cum.shape[1] - 1 :] - cum)
    faded = [
        [(t * fading[first + i : first + i + 1, :]).astype(BF16) for i, t in enumerate(some)]
        for (first, _), some in zip(groups, turned)
    ]
    for (first, count), some, out in zip(groups, faded, outs):
        parts = head_lanes(size, first, count)
        for i, product in enumerate([dot_nn(f, v[:, p]) for f, p in zip(some, parts)]):
            out[i] = product.astype(BF16)


def gate_kernel(groups, slots, q_in, k_in, v_in, bias_in, gate_in, *refs):
    logits_ref, cum_ref, *updates = refs[: 2 + len(groups)]
    q, k, v, bias, gate, sems = refs[2 + len(groups) :]
    pairs = ((gate_in, gate), (bias_in, bias), (k_in, k), (q_in, q), (v_in, v))
    copies = [
        pltpu.make_async_copy(source, target, sems.at[i])
        for i, (source, target) in enumerate(pairs)
    ]
    for copy in copies:
        copy.start()
    width = q.shape[1]
    for copy in copies[:3]:
        copy.wait()
    logits = bias[...] + dot_nt(gate[:, width : 2 * width], k[...])
    copies[3].wait()
    logits = logits + dot_nt(gate[:, :width], q[...])
    copies[4].wait()
    logits = logits + dot_nt(gate[:, 2 * width :], v[...])
    logits_ref[...] = logits
    soft = jnp.maximum(logits, 0.0) + jnp.log1p(jnp.exp(-jnp.abs(logits)))
    cum = exact_dot(-soft, triangle(logits.shape[1], True))
    cum_ref[...] = cum
    if slots > 2:
        add_updates(turn(k, updates[0].shape[1], groups), v, cum, groups, updates)
        return
    opening = lax.axis_index("seq") == 0

    @pl.when(opening)
    def _():
        add_updates(turn(k, updates[0].shape[1], groups), v, cum, groups, updates)

    @pl.when(jnp.logical_not(opening))
    def _():
        for update in updates:
            update[...] = jnp.zeros(update.shape, update.dtype)


def within_kernel(heads, groups, q, k, v, cum_ref, resets, attn_ref, within, rise_ref, *updates):
    rise_ref[...] = (1 - resets[...]).astype(F32) * jnp.exp(cum_ref[...])
    size = q.shape[1] // heads
    if groups:
        add_updates(turn(k, size, groups), v, cum_ref[...], groups, updates)
    cum_columns = cum_ref[...].T
    step = min(heads, STAGE)
    for first in range(0, heads, step):
        count = min(step, heads - first)
        parts = head_lanes(size, first, count)
        scores = [dot_nt(q[:, p], k[:, p]) for p in parts]
        attns = [
            (decay_matrix(cum_columns[:, h : h + 1], cum_ref[h : h + 1, :]) * s).astype(BF16)
            for h, s in enumerate(scores, first)
        ]
        for h, a in enumerate(attns, first):
            attn_ref[h] = a
        for a, p in zip(attns, parts):
            within[:, p] = dot_nn(a, v[:, p])


def mix_kernel(first, count, q, within, cot, rise_ref, state, *refs):
    *forwarded, out, d_mix, pushed, row_ref = refs
    size = state.shape[1]
    opening = lax.axis_index("seq") == 0
    parts, owns = head_lanes(size, first, count), head_lanes(size, 0, count)
    rise = rise_ref[...][first : first + count]
    decays = jnp.where(opening, 0.0, rise).T
    reads = [dot_nn(q[:, p], state[i]) for i, p in enumerate(parts)]
    mixtures = [
        within[:, p] + decays[:, i : i + 1] * x for i, (p, x) in enumerate(zip(parts, reads))
    ]
    upstream = [cot[:, p].astype(F32) for p in parts]
    squares = [jnp.mean(m * m, axis=1, keepdims=True) + EPSILON for m in mixtures]
    shared = [jnp.mean(u * m, axis=1, keepdims=True) for u, m in zip(upstream, mixtures)]
    inverses = [lax.rsqrt(s) for s in squares]
    normed = [m * i for m, i in zip(mixtures, inverses)]
    for n, o in zip(normed, owns):
        out[:, o] = n.astype(BF16)
    grads = [
        ((u - n * (s * i)) * i).astype(BF16)
        for u, n, s, i in zip(upstream, normed, shared, inverses)
    ]
    for g, o in zip(grads, owns):
        d_mix[:, o] = g
    faded = [
        (q[:, p].astype(F32).T * rise[i : i + 1, :]).astype(BF16) for i, p in enumerate(parts)
    ]
    products = [dot_nn(f, g) for f, g in zip(faded, grads)]
    for i, product in enumerate(products):
        product = product.astype(BF16)
        if forwarded:
            product = jnp.where(opening, forwarded[0][i], product)
        pushed[i] = product
    terms = [
        jnp.sum(g.astype(F32) * m, axis=1, keepdims=True) for g, m in zip(grads, mixtures)
    ]
    row_ref[...] = jnp.concatenate(terms, axis=1).T


def members(groups):
    return [(g, i) for g, (_, count) in enumerate(groups) for i in range(count)]


def fading_rows(cum, slots):
    closing = lax.axis_index("seq") == slots - 1
    return jnp.where(closing, 0.0, jnp.exp(cum[:, cum.shape[1] - 1 :] - cum))


def state_terms(keys, moved, fading):
    sums = [jnp.sum(x.astype(F32) * m, axis=1, keepdims=True) for x, m in zip(keys, moved)]
    from_state = jnp.concatenate(sums, axis=1).T * fading
    last = lax.broadcasted_iota(jnp.int32, fading.shape, 1) == fading.shape[1] - 1
    total = jnp.sum(from_state, axis=1, keepdims=True)
    return jnp.where(last, total, 0.0) - from_state


def back_kernel(groups, early, slots, *refs):
    q, k, v, attn, cum_ref, rise_ref = refs[:6]
    number = len(groups)
    outs, d_mixes, states, row_terms = [refs[6 + number * i : 6 + number * (i + 1)] for i in range(4)]
    *grads, output, gq, gk, gv, term_ref, sems = refs[6 + 4 * number :]
    size = states[0].shape[1]
    copies = [
        pltpu.make_async_copy(
            out, output.at[:, pl.ds(first * size, count * size)], sems.at[i]
        )
        for i, ((first, count), out) in enumerate(zip(groups, outs))
    ]
    for copy in copies:
        copy.start()
    cum = cum_ref[...]
    cum_columns = cum.T
    rise_columns = jnp.where(lax.axis_index("seq") == 0, 0.0, rise_ref[...]).T
    fading = fading_rows(cum, slots)
    fading_columns = fading.T
    sums, added = [], []
    places = members(groups)
    for start in range(0, len(places), STAGE):
        some = places[start : start + STAGE]
        heads = range(start, start + len(some))
        parts = head_lanes(size, start, len(some))
        d_outs = [d_mixes[g][:, i * size : (i + 1) * size] for g, i in some]
        columns = [cum_columns[:, h : h + 1] for h in heads]
        d_attns = [dot_nt(d, v[:, p]) for d, p in zip(d_outs, parts)]
        reads = [dot_nt(d, states[g][i]) for d, (g, i) in zip(d_outs, some)]
        weighted = [
            (decay_matrix(c, cum_ref[h : h + 1, :]) * d).astype(BF16)
            for h, c, d in zip(heads, columns, d_attns)
        ]
        ready = [(h, p, g, i) for h, p, (g, i) in zip(heads, parts, some) if g < early]
        moved_k = {h: dot_nt(v[:, p], grads[g][i]) for h, p, g, i in ready}
        moved_v = {h: dot_nn(k[:, p], grads[g][i]) for h, p, g, i in ready}
        for h, p, w, x in zip(heads, parts, weighted, reads):
            gq[:, p] = dot_nn(w, k[:, p]) + rise_columns[:, h : h + 1] * x
        for h, p, w in zip(heads, parts, weighted):
            total = dot_tn(w, q[:, p])
            gk[:, p] = total + fading_columns[:, h : h + 1] * moved_k[h] if h in moved_k else total
        for h, p, d in zip(heads, parts, d_outs):
            total = dot_tn(attn[h], d)
            gv[:, p] = total + fading_columns[:, h : h + 1] * moved_v[h] if h in moved_v else total
        for h, d in zip(heads, d_attns):
            sums.append(jnp.sum(attn[h].astype(F32) * d, axis=0, keepdims=True))
        if ready:
            first = ready[0][0]
            keys = [k[:, p] for _, p, _, _ in ready]
            some_fading = fading[first : first + len(ready)]
            added.append(state_terms(keys, [moved_k[h] for h, *_ in ready], some_fading))
    terms = jnp.concatenate([r[...] for r in row_terms], axis=0) - jnp.concatenate(sums, axis=0)
    if added:
        early_terms = jnp.concatenate(added, axis=0)
        count = early_terms.shape[0]
        term_ref[:count, :] = terms[:count] + early_terms
        term_ref[count:, :] = terms[count:]
    else:
        term_ref[...] = terms
    for copy in copies:
        copy.wait()


def logit_kernel(groups, early, slots, q, k, v, cum_ref, logits_ref, terms, through, *refs):
    late = len(groups) - early
    grads, (d_ref, *outs) = refs[:late], refs[late:]
    size = grads[0].shape[1]
    width = q.shape[1]
    cum = cum_ref[...]
    tokens = cum.shape[1]
    first = groups[early][0]
    parts = head_lanes(size, first, cum.shape[0] - first)
    moved = [dot_nt(v[:, p], grads[g][i]) for p, (g, i) in zip(parts, members(groups[early:]))]
    added = state_terms([k[:, p] for p in parts], moved, fading_rows(cum, slots)[first:])
    d_cum = terms[...] + through[...]
    d_cum = jnp.concatenate([d_cum[:first], d_cum[first:] + added], axis=0) if first else d_cum + added
    d_decay = exact_dot(d_cum, triangle(tokens, False))
    d_logits = (-jax.nn.sigmoid(logits_ref[...]) * d_decay).astype(BF16)
    d_ref[...] = d_logits
    whole = [dot_nn(d_logits, x[...]) for x in (q, k, v)]
    if len(outs) == 1:
        for i in range(3):
            outs[0][:, i * width : (i + 1) * width] = whole[i]
        return
    keep, send, pieces = outs
    joined = jnp.concatenate(whole, axis=1)
    cores, others = pieces.shape[:2]
    piece = 3 * width // (cores * others)
    for j in range(others):
        for c in range(cores):
            row, slot = j // slots * cores + c, j % slots
            pieces[c, j] = pack(joined, (row * slots + slot) * piece, piece).astype(BF16)
    core = lax.axis_index("core")
    keep[...] = pieces[core]
    send[...] = pieces[1 - core]


def pack(joined, first, piece):
    tiles = [joined[:, first + i : first + i + 128] for i in range(0, piece - 127, 128)]
    if piece % 128:
        rest = joined[:, first + piece // 128 * 128 : first + piece]
        half = rest.shape[0] // 2
        tiles.append(jnp.concatenate([rest[:half], rest[half:]], axis=1))
    return jnp.concatenate(tiles, axis=0)


def sum_kernel(arrived, out):
    heads, piece = out.shape
    total = jnp.sum(arrived[...].astype(F32), axis=0)
    tiles = piece // 128
    for i in range(tiles):
        out[:, i * 128 : (i + 1) * 128] = total[i * heads : (i + 1) * heads]
    if piece % 128:
        rest = total[tiles * heads :]
        out[: heads // 2, tiles * 128 :] = rest[:, :64]
        out[heads // 2 :, tiles * 128 :] = rest[:, 64:]


def finish_kernel(groups, early, slots, gq, gk, gv, k, v, cum_ref, d_logits, gate, *refs):
    late = len(groups) - early
    grads, outs, (result, sems) = refs[:late], refs[late : late + 3], refs[late + 3 :]
    width = gq.shape[1]
    places = members(groups)
    size = width // len(places)
    fading = fading_rows(cum_ref[...], slots).T
    copies = []
    for index, (partial, operand) in enumerate(((gq, None), (gk, v), (gv, k))):
        for start in range(0, len(places), STAGE):
            some = places[start : start + STAGE]
            at = index * width + start * size
            back = dot_tn(d_logits[...], gate[:, at : at + len(some) * size])
            parts, owns = head_lanes(size, start, len(some)), head_lanes(size, 0, len(some))
            moved = {}
            for h, (p, (g, i)) in enumerate(zip(parts, some), start):
                if operand is not None and g >= early:
                    dot = dot_nt if index == 1 else dot_nn
                    moved[h] = dot(operand[:, p], grads[g - early][i])
            for h, (p, o) in enumerate(zip(parts, owns), start):
                total = partial[:, p] + back[:, o]
                if h in moved:
                    total = total + fading[:, h : h + 1] * moved[h]
                result[index, :, p] = total.astype(BF16)
            lanes = pl.ds(start * size, len(some) * size)
            copies.append(
                pltpu.make_async_copy(
                    result.at[index, :, lanes], outs[index].at[:, lanes], sems.at[len(copies)]
                )
            )
            copies[-1].start()
    for copy in copies:
        copy.wait()


def shape(dims, dtype):
    return jax.ShapeDtypeStruct(dims, dtype)


def head_groups(heads):
    sizes=[3, 3, 2, 3, 3, 2]
    parts=len(sizes)
    return [(sum(sizes[:i]), sizes[i]) for i in range(parts)]


def body(
    pairs, cores, seq_size, queries, keys, values, decay_bias, gate_matrix, resets, cotangent
):
    q, k, v, cot = queries[0], keys[0], values[0], cotangent[0]
    tokens, width = q.shape
    heads = decay_bias.shape[1]
    size = width // heads
    gate = gate_matrix.T
    groups = head_groups(heads)
    forward = [(i, i + 1) for i in range(seq_size - 1)]
    backward = [(i + 1, i) for i in range(seq_size - 1)]
    kept = (1 - resets[0, 0]).astype(F32)

    def state_shapes(some):
        return tuple(shape((count, size, size), BF16) for _, count in some)

    ahead = 3 if seq_size == 2 and len(groups) > 2 else len(groups)
    logits, cum, *updates = pl.pallas_call(
        functools.partial(gate_kernel, groups[:ahead], seq_size),
        out_shape=(shape((heads, tokens), F32),) * 2
        + state_shapes(groups[:ahead]),
        in_specs=[hbm()] * 5,
        out_specs=(spec(),) * (2 + ahead),
        scratch_shapes=[
            pltpu.VMEM((tokens, width), BF16),
            pltpu.VMEM((tokens, width), BF16),
            pltpu.VMEM((tokens, width), BF16),
            pltpu.VMEM((heads, tokens), F32),
            pltpu.VMEM((heads, 3 * width), BF16),
            pltpu.SemaphoreType.DMA((5,)),
        ],
        compiler_params=params(VMEM_FULL),
        cost_estimate=cost(),
        name="gate",
    )(q, k, v, decay_bias[0], gate)
    attn, within, rise, *made = pl.pallas_call(
        functools.partial(within_kernel, heads, groups[ahead:]),
        out_shape=(
            shape((heads, tokens, tokens), BF16),
            shape((tokens, width), F32),
            shape((heads, tokens), F32),
        )
        + state_shapes(groups[ahead:]),
        in_specs=[spec()] * 5,
        out_specs=(spec(),) * (3 + len(groups) - ahead),
        compiler_params=params(),
        cost_estimate=cost(),
        name="within",
    )(q, k, v, cum, resets)
    updates += made

    def chain(own, first, count, pairs):
        if seq_size == 2:
            return lax.ppermute(own, "seq", [(0, 1), (1, 0)])
        arrived = lax.ppermute(own, "seq", pairs)
        for _ in range(seq_size - 2):
            factor = kept * jnp.exp(cum[first : first + count, -1])[:, None, None]
            passed = factor * arrived.astype(F32) + own.astype(F32)
            arrived = lax.ppermute(passed.astype(BF16), "seq", pairs)
        return arrived

    entering = [chain(updates[g], *groups[g], forward) for g in range(ahead)]
    outs, d_mixes, rows, grads = [], [], [], []
    for g, (first, count) in enumerate(groups):
        forwarded = [updates[g + ahead]] if g + ahead < len(groups) else []
        out_g, d_g, pushed, rows_g = pl.pallas_call(
            functools.partial(mix_kernel, first, count),
            out_shape=(
                shape((tokens, count * size), BF16),
                shape((tokens, count * size), BF16),
                shape((count, size, size), BF16),
                shape((count, tokens), F32),
            ),
            in_specs=[spec()] * (5 + len(forwarded)),
            out_specs=(spec(),) * 4,
            compiler_params=params(),
            cost_estimate=cost(),
            name="mix",
        )(q, within, cot, rise, entering[g], *forwarded)
        outs.append(out_g)
        d_mixes.append(d_g)
        rows.append(rows_g)
        if forwarded:
            arrived = lax.ppermute(pushed, "seq", [(0, 1), (1, 0)])
            entering.append(arrived)
            grads.append(arrived)
        else:
            grads.append(chain(pushed, first, count, backward))

    early = min(ahead, len(groups) // 2)
    output, gq, gk, gv, terms = pl.pallas_call(
        functools.partial(back_kernel, groups, early, seq_size),
        out_shape=(shape((tokens, width), BF16),)
        + (shape((tokens, width), F32),) * 3
        + (shape((heads, tokens), F32),),
        in_specs=[spec()] * (6 + 4 * len(groups) + early),
        out_specs=(hbm(),) + (spec(),) * 4,
        scratch_shapes=[pltpu.SemaphoreType.DMA((len(groups),))],
        compiler_params=params(),
        cost_estimate=cost(),
        name="back",
    )(q, k, v, attn, cum, rise, *outs, *d_mixes, *entering, *rows, *grads[:early])
    if seq_size > 2:
        through = [
            kept * jnp.sum(g.astype(F32) * s.astype(F32), axis=(1, 2))[:, None]
            for g, s in zip(grads, entering)
        ]
        through = jnp.concatenate(through, axis=0) * jnp.exp(cum[:, -1:])
        through = through * (jnp.arange(tokens) == tokens - 1).astype(F32)
    else:
        through = jnp.zeros((heads, tokens), F32)

    piece = 3 * width // (pairs * CORES * seq_size)
    exchanged = cores == CORES and piece >= 128 and piece % 64 == 0 and heads % 16 == 0
    others = pairs * seq_size
    packed = piece * heads // 128
    if exchanged:
        part_shapes = (shape((others, packed, 128), BF16),) * 2
        scratch = [pltpu.VMEM((CORES, others, packed, 128), BF16)]
    else:
        part_shapes = (shape((heads, 3 * width), F32),)
        scratch = []
    d_logits, *parts = pl.pallas_call(
        functools.partial(logit_kernel, groups, early, seq_size),
        out_shape=(shape((heads, tokens), BF16),) + part_shapes,
        in_specs=[spec()] * (7 + len(groups) - early),
        out_specs=(spec(),) * (1 + len(part_shapes)),
        scratch_shapes=scratch,
        compiler_params=params(),
        cost_estimate=cost(),
        name="logits",
    )(q, k, v, cum, logits, terms, through, *grads[early:])

    input_grads = pl.pallas_call(
        functools.partial(finish_kernel, groups, early, seq_size),
        out_shape=(shape((tokens, width), BF16),) * 3,
        in_specs=[spec()] * (8 + len(groups) - early),
        out_specs=(hbm(),) * 3,
        scratch_shapes=[
            pltpu.VMEM((3, tokens, width), BF16),
            pltpu.SemaphoreType.DMA((3 * -(-heads // STAGE),)),
        ],
        compiler_params=params(),
        cost_estimate=cost(),
        name="finish",
    )(gq, gk, gv, k, v, cum, d_logits, gate, *grads[early:])

    if exchanged:
        keep, send = parts
        arrived = lax.ppermute(send, "core", [(0, 1), (1, 0)])
        total = (keep.astype(F32) + arrived.astype(F32)).astype(BF16)
        total, *input_grads = lax.optimization_barrier((total, *input_grads))
        arrived = lax.all_to_all(total, ("pair", "seq"), 0, 0, tiled=True)
        grad_gate = pl.pallas_call(
            sum_kernel,
            out_shape=shape((heads, piece), F32),
            in_specs=[spec()],
            out_specs=spec(),
            compiler_params=params(),
            name="sum",
        )(arrived).T
    else:
        grad_gate = lax.psum_scatter(
            parts[0].T, ("pair", "core", "seq"), scatter_dimension=0, tiled=True
        )
    return output[None], *[g[None] for g in input_grads], grad_gate


def solution(mesh):
    rows, slots = mesh.devices.shape
    cores = CORES if rows % CORES == 0 else 1
    devices = mesh.devices.reshape(rows // cores, cores, slots)
    mesh = jax.sharding.Mesh(devices, ("pair", "core", "seq"))
    row = ("pair", "core")
    tokens = P(row, "seq", None)
    return jax.shard_map(
        functools.partial(body, rows // cores, cores, slots),
        mesh=mesh,
        in_specs=(tokens, tokens, tokens, P(row, None, "seq"), P(), P(row, "seq"), tokens),
        out_specs=(tokens, tokens, tokens, tokens, P((*row, "seq"), None)),
        check_vma=False,
    )
```

```python
import functools

import jax
import jax.numpy as jnp
from jax import lax
from jax.experimental import pallas as pl
from jax.experimental.pallas import tpu as pltpu
from jax.sharding import PartitionSpec as P

EPSILON = 1e-06
F32 = jnp.float32
BF16 = jnp.bfloat16
STAGE = 8
CORES = 2
VMEM_LIMIT = 16 * 1024 * 1024
VMEM_FULL = 58 * 1024 * 1024


def dot_nn(a, b):
    return lax.dot_general(a, b, (((1,), (0,)), ((), ())), preferred_element_type=F32)


def dot_nt(a, b):
    return lax.dot_general(a, b, (((1,), (1,)), ((), ())), preferred_element_type=F32)


def dot_tn(a, b):
    return lax.dot_general(a, b, (((0,), (0,)), ((), ())), preferred_element_type=F32)


def exact_dot(x, ones):
    rows = x.shape[0]
    high = x.astype(BF16)
    rest = x - high.astype(F32)
    middle = rest.astype(BF16)
    low = (rest - middle.astype(F32)).astype(BF16)
    parts = dot_nn(jnp.concatenate([high, middle, low], axis=0), ones)
    return parts[:rows] + parts[rows : 2 * rows] + parts[2 * rows :]


def triangle(size, upper):
    rows = lax.broadcasted_iota(jnp.int32, (size, size), 0)
    columns = lax.broadcasted_iota(jnp.int32, (size, size), 1)
    keep = rows <= columns if upper else rows >= columns
    return jnp.where(keep, 1.0, 0.0).astype(BF16)


def decay_matrix(cum_column, cum_row):
    size = cum_row.shape[1]
    rows = lax.broadcasted_iota(jnp.int32, (size, size), 0)
    columns = lax.broadcasted_iota(jnp.int32, (size, size), 1)
    return jnp.exp(jnp.where(columns <= rows, cum_column - cum_row, -jnp.inf))


def spec():
    return pl.BlockSpec(memory_space=pltpu.VMEM)


def smem():
    return pl.BlockSpec(memory_space=pltpu.SMEM)


def hbm():
    return pl.BlockSpec(memory_space=pltpu.HBM)


def params(limit=VMEM_LIMIT):
    return pltpu.CompilerParams(vmem_limit_bytes=limit)


def cost():
    return pl.CostEstimate(flops=1000, bytes_accessed=1000, transcendentals=0)


def head_lanes(size, first, count):
    return [slice(h * size, (h + 1) * size) for h in range(first, first + count)]


def turn(k, size, groups):
    return [
        [k[:, p].astype(F32).T for p in head_lanes(size, first, count)] for first, count in groups
    ]


def add_updates(turned, v, cum, groups, outs):
    size = outs[0].shape[1]
    fading = jnp.exp(cum[:, cum.shape[1] - 1 :] - cum)
    faded = [
        [(t * fading[first + i : first + i + 1, :]).astype(BF16) for i, t in enumerate(some)]
        for (first, _), some in zip(groups, turned)
    ]
    for (first, count), some, out in zip(groups, faded, outs):
        parts = head_lanes(size, first, count)
        for i, product in enumerate([dot_nn(f, v[:, p]) for f, p in zip(some, parts)]):
            out[i] = product.astype(BF16)


def cumulate(logits):
    soft = jnp.maximum(logits, 0.0) + jnp.log1p(jnp.exp(-jnp.abs(logits)))
    return exact_dot(-soft, triangle(logits.shape[1], True))


def gate_kernel(groups, slots, q_in, k_in, v_in, bias_in, gate_in, *refs):
    logits_ref, *updates = refs[: 1 + len(groups)]
    q, k, v, bias, gate, sems = refs[1 + len(groups) :]
    pairs = ((gate_in, gate), (bias_in, bias), (k_in, k), (q_in, q), (v_in, v))
    copies = [
        pltpu.make_async_copy(source, target, sems.at[i])
        for i, (source, target) in enumerate(pairs)
    ]
    for copy in copies:
        copy.start()
    width = q.shape[1]
    for copy in copies[:3]:
        copy.wait()
    logits = bias[...] + dot_nt(gate[:, width : 2 * width], k[...])
    copies[3].wait()
    logits = logits + dot_nt(gate[:, :width], q[...])
    copies[4].wait()
    logits = logits + dot_nt(gate[:, 2 * width :], v[...])
    logits_ref[...] = logits

    def run():
        turned = turn(k, updates[0].shape[1], groups)
        add_updates(turned, v, cumulate(logits), groups, updates)

    if slots > 2:
        run()
        return
    opening = lax.axis_index("seq") == 0
    pl.when(opening)(run)

    @pl.when(jnp.logical_not(opening))
    def _():
        for update in updates:
            update[...] = jnp.zeros(update.shape, update.dtype)


def within_kernel(heads, groups, q, k, v, logits, resets, cum_ref, attn_ref, within, rise_ref, *updates):
    cum = cumulate(logits[...])
    cum_ref[...] = cum
    rise_ref[...] = (1 - resets[...]).astype(F32) * jnp.exp(cum)
    size = q.shape[1] // heads
    if groups:
        add_updates(turn(k, size, groups), v, cum, groups, updates)
    cum_columns = cum.T
    step = min(heads, STAGE)
    for first in range(0, heads, step):
        count = min(step, heads - first)
        parts = head_lanes(size, first, count)
        scores = [dot_nt(q[:, p], k[:, p]) for p in parts]
        attns = [
            (decay_matrix(cum_columns[:, h : h + 1], cum[h : h + 1, :]) * s).astype(BF16)
            for h, s in enumerate(scores, first)
        ]
        for h, a in enumerate(attns, first):
            attn_ref[h] = a
        for a, p in zip(attns, parts):
            within[:, p] = dot_nn(a, v[:, p])


def mix_kernel(first, count, q, within, cot, rise_ref, state, *refs):
    *forwarded, out, d_mix, pushed, row_ref = refs
    size = state.shape[1]
    opening = lax.axis_index("seq") == 0
    parts, owns = head_lanes(size, first, count), head_lanes(size, 0, count)
    rise = rise_ref[...][first : first + count]
    decays = jnp.where(opening, 0.0, rise).T
    reads = [dot_nn(q[:, p], state[i]) for i, p in enumerate(parts)]
    mixtures = [
        within[:, p] + decays[:, i : i + 1] * x for i, (p, x) in enumerate(zip(parts, reads))
    ]
    upstream = [cot[:, p].astype(F32) for p in parts]
    squares = [jnp.mean(m * m, axis=1, keepdims=True) + EPSILON for m in mixtures]
    shared = [jnp.mean(u * m, axis=1, keepdims=True) for u, m in zip(upstream, mixtures)]
    inverses = [lax.rsqrt(s) for s in squares]
    normed = [m * i for m, i in zip(mixtures, inverses)]
    for n, o in zip(normed, owns):
        out[:, o] = n.astype(BF16)
    grads = [
        ((u - n * (s * i)) * i).astype(BF16)
        for u, n, s, i in zip(upstream, normed, shared, inverses)
    ]
    for g, o in zip(grads, owns):
        d_mix[:, o] = g
    faded = [
        (q[:, p].astype(F32).T * rise[i : i + 1, :]).astype(BF16) for i, p in enumerate(parts)
    ]
    products = [dot_nn(f, g) for f, g in zip(faded, grads)]
    for i, product in enumerate(products):
        product = product.astype(BF16)
        if forwarded:
            product = jnp.where(opening, forwarded[0][i], product)
        pushed[i] = product
    terms = [
        jnp.sum(g.astype(F32) * m, axis=1, keepdims=True) for g, m in zip(grads, mixtures)
    ]
    row_ref[...] = jnp.concatenate(terms, axis=1).T


def members(groups):
    return [(g, i) for g, (_, count) in enumerate(groups) for i in range(count)]


def fading_rows(cum, slots):
    closing = lax.axis_index("seq") == slots - 1
    return jnp.where(closing, 0.0, jnp.exp(cum[:, cum.shape[1] - 1 :] - cum))


def state_terms(keys, moved, fading):
    sums = [jnp.sum(x.astype(F32) * m, axis=1, keepdims=True) for x, m in zip(keys, moved)]
    from_state = jnp.concatenate(sums, axis=1).T * fading
    last = lax.broadcasted_iota(jnp.int32, fading.shape, 1) == fading.shape[1] - 1
    total = jnp.sum(from_state, axis=1, keepdims=True)
    return jnp.where(last, total, 0.0) - from_state


def back_kernel(groups, early, slots, *refs):
    q, k, v, attn, cum_ref, rise_ref = refs[:6]
    number = len(groups)
    outs, d_mixes, states, row_terms = [refs[6 + number * i : 6 + number * (i + 1)] for i in range(4)]
    *grads, output, gq, gk, gv, term_ref, sems = refs[6 + 4 * number :]
    size = states[0].shape[1]
    copies = [
        pltpu.make_async_copy(
            out, output.at[:, pl.ds(first * size, count * size)], sems.at[i]
        )
        for i, ((first, count), out) in enumerate(zip(groups, outs))
    ]
    for copy in copies:
        copy.start()
    cum = cum_ref[...]
    cum_columns = cum.T
    rise_columns = jnp.where(lax.axis_index("seq") == 0, 0.0, rise_ref[...]).T
    fading = fading_rows(cum, slots)
    fading_columns = fading.T
    sums, added = [], []
    places = members(groups)
    for start in range(0, len(places), STAGE):
        some = places[start : start + STAGE]
        heads = range(start, start + len(some))
        parts = head_lanes(size, start, len(some))
        d_outs = [d_mixes[g][:, i * size : (i + 1) * size] for g, i in some]
        columns = [cum_columns[:, h : h + 1] for h in heads]
        d_attns = [dot_nt(d, v[:, p]) for d, p in zip(d_outs, parts)]
        reads = [dot_nt(d, states[g][i]) for d, (g, i) in zip(d_outs, some)]
        weighted = [
            (decay_matrix(c, cum_ref[h : h + 1, :]) * d).astype(BF16)
            for h, c, d in zip(heads, columns, d_attns)
        ]
        ready = [(h, p, g, i) for h, p, (g, i) in zip(heads, parts, some) if g < early]
        moved_k = {h: dot_nt(v[:, p], grads[g][i]) for h, p, g, i in ready}
        moved_v = {h: dot_nn(k[:, p], grads[g][i]) for h, p, g, i in ready}
        for h, p, w, x in zip(heads, parts, weighted, reads):
            gq[:, p] = dot_nn(w, k[:, p]) + rise_columns[:, h : h + 1] * x
        for h, p, w in zip(heads, parts, weighted):
            total = dot_tn(w, q[:, p])
            gk[:, p] = total + fading_columns[:, h : h + 1] * moved_k[h] if h in moved_k else total
        for h, p, d in zip(heads, parts, d_outs):
            total = dot_tn(attn[h], d)
            gv[:, p] = total + fading_columns[:, h : h + 1] * moved_v[h] if h in moved_v else total
        for h, d in zip(heads, d_attns):
            sums.append(jnp.sum(attn[h].astype(F32) * d, axis=0, keepdims=True))
        if ready:
            first = ready[0][0]
            keys = [k[:, p] for _, p, _, _ in ready]
            some_fading = fading[first : first + len(ready)]
            added.append(state_terms(keys, [moved_k[h] for h, *_ in ready], some_fading))
    terms = jnp.concatenate([r[...] for r in row_terms], axis=0) - jnp.concatenate(sums, axis=0)
    if added:
        early_terms = jnp.concatenate(added, axis=0)
        count = early_terms.shape[0]
        term_ref[:count, :] = terms[:count] + early_terms
        term_ref[count:, :] = terms[count:]
    else:
        term_ref[...] = terms
    for copy in copies:
        copy.wait()


def logit_kernel(groups, early, slots, q, k, v, cum_ref, logits_ref, terms, *refs):
    late = len(groups) - early
    through, refs = (refs[0], refs[1:]) if slots > 2 else (None, refs)
    grads, (d_ref, *outs) = refs[:late], refs[late:]
    size = grads[0].shape[1]
    width = q.shape[1]
    cum = cum_ref[...]
    tokens = cum.shape[1]
    first = groups[early][0]
    parts = head_lanes(size, first, cum.shape[0] - first)
    moved = [dot_nt(v[:, p], grads[g][i]) for p, (g, i) in zip(parts, members(groups[early:]))]
    added = state_terms([k[:, p] for p in parts], moved, fading_rows(cum, slots)[first:])
    d_cum = terms[...] if through is None else terms[...] + through[...]
    d_cum = jnp.concatenate([d_cum[:first], d_cum[first:] + added], axis=0) if first else d_cum + added
    d_decay = exact_dot(d_cum, triangle(tokens, False))
    d_logits = (-jax.nn.sigmoid(logits_ref[...]) * d_decay).astype(BF16)
    d_ref[...] = d_logits
    whole = [dot_nn(d_logits, x[...]) for x in (q, k, v)]
    if len(outs) == 1:
        for i in range(3):
            outs[0][:, i * width : (i + 1) * width] = whole[i]
        return
    keep, send, pieces = outs
    joined = jnp.concatenate(whole, axis=1)
    cores, others = pieces.shape[:2]
    piece = 3 * width // (cores * others)
    packed = pack(joined, piece, cores * others)
    for j in range(others):
        for c in range(cores):
            row, slot = j // slots * cores + c, j % slots
            pieces[c, j] = packed[row * slots + slot]
    core = lax.axis_index("core")
    keep[...] = pieces[core]
    send[...] = pieces[1 - core]


def pack(joined, piece, count):
    heads, width = joined.shape
    half = heads // 2
    low = lax.broadcasted_iota(jnp.int32, (half, 128), 1) < 64
    behind = pltpu.roll(joined, width - 64, axis=1)
    ahead = pltpu.roll(joined, 64, axis=1)
    packed = []
    for i in range(count):
        at = i * piece // 128 * 128
        source, other = (joined, ahead) if i * piece == at else (behind, joined)
        tiles = [source[:, at + n : at + n + 128] for n in range(0, piece - 127, 128)]
        if piece % 128:
            at += piece // 128 * 128
            lower, upper = source[:half, at : at + 128], other[half:, at : at + 128]
            tiles.append(jnp.where(low, lower, upper))
        packed.append(jnp.concatenate(tiles, axis=0).astype(BF16))
    return packed


def sum_kernel(arrived, out):
    heads, piece = out.shape
    total = jnp.sum(arrived[...].astype(F32), axis=0)
    tiles = piece // 128
    for i in range(tiles):
        out[:, i * 128 : (i + 1) * 128] = total[i * heads : (i + 1) * heads]
    if piece % 128:
        rest = total[tiles * heads :]
        out[: heads // 2, tiles * 128 :] = rest[:, :64]
        out[heads // 2 :, tiles * 128 :] = rest[:, 64:]


def finish_kernel(groups, early, slots, gq, gk, gv, k, v, cum_ref, d_logits, gate, *refs):
    late = len(groups) - early
    grads, outs, (result, sems) = refs[:late], refs[late : late + 3], refs[late + 3 :]
    width = gq.shape[1]
    places = members(groups)
    size = width // len(places)
    fading = fading_rows(cum_ref[...], slots).T
    copies = []
    for index, (partial, operand) in enumerate(((gq, None), (gk, v), (gv, k))):
        for start in range(0, len(places), STAGE):
            some = places[start : start + STAGE]
            at = index * width + start * size
            back = dot_tn(d_logits[...], gate[:, at : at + len(some) * size])
            parts, owns = head_lanes(size, start, len(some)), head_lanes(size, 0, len(some))
            moved = {}
            for h, (p, (g, i)) in enumerate(zip(parts, some), start):
                if operand is not None and g >= early:
                    dot = dot_nt if index == 1 else dot_nn
                    moved[h] = dot(operand[:, p], grads[g - early][i])
            for h, (p, o) in enumerate(zip(parts, owns), start):
                total = partial[:, p] + back[:, o]
                if h in moved:
                    total = total + fading[:, h : h + 1] * moved[h]
                result[index, :, p] = total.astype(BF16)
            lanes = pl.ds(start * size, len(some) * size)
            copies.append(
                pltpu.make_async_copy(
                    result.at[index, :, lanes], outs[index].at[:, lanes], sems.at[len(copies)]
                )
            )
            copies[-1].start()
    for copy in copies:
        copy.wait()


def shape(dims, dtype):
    return jax.ShapeDtypeStruct(dims, dtype)


def head_groups(heads):
    half = heads // 2
    sizes = [half // 3 + (1 if i < half % 3 else 0) for i in range(3)] * 2
    return [(sum(sizes[:i]), size) for i, size in enumerate(sizes)]


def body(
    pairs, cores, seq_size, queries, keys, values, decay_bias, gate_matrix, resets, cotangent
):
    q, k, v, cot = queries[0], keys[0], values[0], cotangent[0]
    tokens, width = q.shape
    heads = decay_bias.shape[1]
    size = width // heads
    gate = gate_matrix.T
    groups = head_groups(heads)
    forward = [(i, i + 1) for i in range(seq_size - 1)]
    backward = [(i + 1, i) for i in range(seq_size - 1)]
    kept = (1 - resets[0, 0]).astype(F32)

    def state_shapes(some):
        return tuple(shape((count, size, size), BF16) for _, count in some)

    ahead = 3 if seq_size == 2 and len(groups) > 2 else len(groups)
    logits, *updates = pl.pallas_call(
        functools.partial(gate_kernel, groups[:ahead], seq_size),
        out_shape=(shape((heads, tokens), F32),) + state_shapes(groups[:ahead]),
        in_specs=[hbm()] * 5,
        out_specs=(spec(),) * (1 + ahead),
        scratch_shapes=[
            pltpu.VMEM((tokens, width), BF16),
            pltpu.VMEM((tokens, width), BF16),
            pltpu.VMEM((tokens, width), BF16),
            pltpu.VMEM((heads, tokens), F32),
            pltpu.VMEM((heads, 3 * width), BF16),
            pltpu.SemaphoreType.DMA((5,)),
        ],
        compiler_params=params(VMEM_FULL),
        cost_estimate=cost(),
        name="gate",
    )(q, k, v, decay_bias[0], gate)
    cum, attn, within, rise, *made = pl.pallas_call(
        functools.partial(within_kernel, heads, groups[ahead:]),
        out_shape=(
            shape((heads, tokens), F32),
            shape((heads, tokens, tokens), BF16),
            shape((tokens, width), F32),
            shape((heads, tokens), F32),
        )
        + state_shapes(groups[ahead:]),
        in_specs=[spec()] * 5,
        out_specs=(spec(),) * (4 + len(groups) - ahead),
        compiler_params=params(),
        cost_estimate=cost(),
        name="within",
    )(q, k, v, logits, resets)
    updates += made

    def chain(own, first, count, pairs):
        if seq_size == 2:
            return lax.ppermute(own, "seq", [(0, 1), (1, 0)])
        arrived = lax.ppermute(own, "seq", pairs)
        for _ in range(seq_size - 2):
            factor = kept * jnp.exp(cum[first : first + count, -1])[:, None, None]
            passed = factor * arrived.astype(F32) + own.astype(F32)
            arrived = lax.ppermute(passed.astype(BF16), "seq", pairs)
        return arrived

    entering = [chain(updates[g], *groups[g], forward) for g in range(ahead)]
    outs, d_mixes, rows, grads = [], [], [], []
    for g, (first, count) in enumerate(groups):
        forwarded = [updates[g + ahead]] if g + ahead < len(groups) else []
        out_g, d_g, pushed, rows_g = pl.pallas_call(
            functools.partial(mix_kernel, first, count),
            out_shape=(
                shape((tokens, count * size), BF16),
                shape((tokens, count * size), BF16),
                shape((count, size, size), BF16),
                shape((count, tokens), F32),
            ),
            in_specs=[spec()] * (5 + len(forwarded)),
            out_specs=(spec(),) * 4,
            compiler_params=params(),
            cost_estimate=cost(),
            name="mix",
        )(q, within, cot, rise, entering[g], *forwarded)
        outs.append(out_g)
        d_mixes.append(d_g)
        rows.append(rows_g)
        if forwarded:
            arrived = lax.ppermute(pushed, "seq", [(0, 1), (1, 0)])
            entering.append(arrived)
            grads.append(arrived)
        else:
            grads.append(chain(pushed, first, count, backward))

    early = min(ahead, len(groups) // 2)
    output, gq, gk, gv, terms = pl.pallas_call(
        functools.partial(back_kernel, groups, early, seq_size),
        out_shape=(shape((tokens, width), BF16),)
        + (shape((tokens, width), F32),) * 3
        + (shape((heads, tokens), F32),),
        in_specs=[spec()] * (6 + 4 * len(groups) + early),
        out_specs=(hbm(),) + (spec(),) * 4,
        scratch_shapes=[pltpu.SemaphoreType.DMA((len(groups),))],
        compiler_params=params(),
        cost_estimate=cost(),
        name="back",
    )(q, k, v, attn, cum, rise, *outs, *d_mixes, *entering, *rows, *grads[:early])
    through = []
    if seq_size > 2:
        products = [
            kept * jnp.sum(g.astype(F32) * s.astype(F32), axis=(1, 2))[:, None]
            for g, s in zip(grads, entering)
        ]
        ends = jnp.concatenate(products, axis=0) * jnp.exp(cum[:, -1:])
        through = [ends * (jnp.arange(tokens) == tokens - 1).astype(F32)]

    piece = 3 * width // (pairs * CORES * seq_size)
    exchanged = cores == CORES and piece >= 128 and piece % 64 == 0 and heads % 16 == 0
    others = pairs * seq_size
    packed = piece * heads // 128
    if exchanged:
        part_shapes = (shape((others, packed, 128), BF16),) * 2
        scratch = [pltpu.VMEM((CORES, others, packed, 128), BF16)]
    else:
        part_shapes = (shape((heads, 3 * width), F32),)
        scratch = []
    d_logits, *parts = pl.pallas_call(
        functools.partial(logit_kernel, groups, early, seq_size),
        out_shape=(shape((heads, tokens), BF16),) + part_shapes,
        in_specs=[spec()] * (6 + len(through) + len(groups) - early),
        out_specs=(spec(),) * (1 + len(part_shapes)),
        scratch_shapes=scratch,
        compiler_params=params(),
        cost_estimate=cost(),
        name="logits",
    )(q, k, v, cum, logits, terms, *through, *grads[early:])

    input_grads = pl.pallas_call(
        functools.partial(finish_kernel, groups, early, seq_size),
        out_shape=(shape((tokens, width), BF16),) * 3,
        in_specs=[spec()] * (8 + len(groups) - early),
        out_specs=(hbm(),) * 3,
        scratch_shapes=[
            pltpu.VMEM((3, tokens, width), BF16),
            pltpu.SemaphoreType.DMA((3 * -(-heads // STAGE),)),
        ],
        compiler_params=params(),
        cost_estimate=cost(),
        name="finish",
    )(gq, gk, gv, k, v, cum, d_logits, gate, *grads[early:])

    if exchanged:
        keep, send = parts
        arrived = lax.ppermute(send, "core", [(0, 1), (1, 0)])
        total = (keep.astype(F32) + arrived.astype(F32)).astype(BF16)
        total, *input_grads = lax.optimization_barrier((total, *input_grads))
        arrived = lax.all_to_all(total, ("pair", "seq"), 0, 0, tiled=True)
        grad_gate = pl.pallas_call(
            sum_kernel,
            out_shape=shape((heads, piece), F32),
            in_specs=[spec()],
            out_specs=spec(),
            compiler_params=params(),
            name="sum",
        )(arrived).T
    else:
        grad_gate = lax.psum_scatter(
            parts[0].T, ("pair", "core", "seq"), scatter_dimension=0, tiled=True
        )
    return output[None], *[g[None] for g in input_grads], grad_gate


def solution(mesh):
    rows, slots = mesh.devices.shape
    cores = CORES if rows % CORES == 0 else 1
    devices = mesh.devices.reshape(rows // cores, cores, slots)
    mesh = jax.sharding.Mesh(devices, ("pair", "core", "seq"))
    row = ("pair", "core")
    tokens = P(row, "seq", None)
    return jax.shard_map(
        functools.partial(body, rows // cores, cores, slots),
        mesh=mesh,
        in_specs=(tokens, tokens, tokens, P(row, None, "seq"), P(), P(row, "seq"), tokens),
        out_specs=(tokens, tokens, tokens, tokens, P((*row, "seq"), None)),
        check_vma=False,
    )
```

```python
import functools

import jax
import jax.numpy as jnp
from jax import lax
from jax.experimental import pallas as pl
from jax.experimental.pallas import tpu as pltpu
from jax.sharding import PartitionSpec as P

EPSILON = 1e-06
F32 = jnp.float32
BF16 = jnp.bfloat16
STAGE = 8
CORES = 2
VMEM_LIMIT = 16 * 1024 * 1024
VMEM_FULL = 58 * 1024 * 1024


def dot_nn(a, b):
    return lax.dot_general(a, b, (((1,), (0,)), ((), ())), preferred_element_type=F32)


def dot_nt(a, b):
    return lax.dot_general(a, b, (((1,), (1,)), ((), ())), preferred_element_type=F32)


def dot_tn(a, b):
    return lax.dot_general(a, b, (((0,), (0,)), ((), ())), preferred_element_type=F32)


def exact_dot(x, ones):
    rows = x.shape[0]
    high = x.astype(BF16)
    rest = x - high.astype(F32)
    middle = rest.astype(BF16)
    low = (rest - middle.astype(F32)).astype(BF16)
    parts = dot_nn(jnp.concatenate([high, middle, low], axis=0), ones)
    return parts[:rows] + parts[rows : 2 * rows] + parts[2 * rows :]


def triangle(size, upper):
    rows = lax.broadcasted_iota(jnp.int32, (size, size), 0)
    columns = lax.broadcasted_iota(jnp.int32, (size, size), 1)
    keep = rows <= columns if upper else rows >= columns
    return jnp.where(keep, 1.0, 0.0).astype(BF16)


def decay_matrix(cum_column, cum_row):
    size = cum_row.shape[1]
    rows = lax.broadcasted_iota(jnp.int32, (size, size), 0)
    columns = lax.broadcasted_iota(jnp.int32, (size, size), 1)
    return jnp.exp(jnp.where(columns <= rows, cum_column - cum_row, -jnp.inf))


def spec():
    return pl.BlockSpec(memory_space=pltpu.VMEM)


def smem():
    return pl.BlockSpec(memory_space=pltpu.SMEM)


def hbm():
    return pl.BlockSpec(memory_space=pltpu.HBM)


def params(limit=VMEM_LIMIT):
    return pltpu.CompilerParams(vmem_limit_bytes=limit)


def cost():
    return pl.CostEstimate(flops=1000, bytes_accessed=1000, transcendentals=0)


def head_lanes(size, first, count):
    return [slice(h * size, (h + 1) * size) for h in range(first, first + count)]


def turn(k, size, groups):
    return [
        [k[:, p].astype(F32).T for p in head_lanes(size, first, count)] for first, count in groups
    ]


def add_updates(turned, v, cum, groups, outs):
    size = outs[0].shape[1]
    fading = jnp.exp(cum[:, cum.shape[1] - 1 :] - cum)
    faded = [
        [(t * fading[first + i : first + i + 1, :]).astype(BF16) for i, t in enumerate(some)]
        for (first, _), some in zip(groups, turned)
    ]
    for (first, count), some, out in zip(groups, faded, outs):
        parts = head_lanes(size, first, count)
        for i, product in enumerate([dot_nn(f, v[:, p]) for f, p in zip(some, parts)]):
            out[i] = product.astype(BF16)


def cumulate(logits):
    soft = jnp.maximum(logits, 0.0) + jnp.log1p(jnp.exp(-jnp.abs(logits)))
    return exact_dot(-soft, triangle(logits.shape[1], True))


def gate_kernel(groups, slots, q_in, k_in, v_in, bias_in, gate_in, *refs):
    logits_ref, *updates = refs[: 1 + len(groups)]
    q, k, v, bias, gate, sems = refs[1 + len(groups) :]
    pairs = ((gate_in, gate), (bias_in, bias), (k_in, k), (q_in, q), (v_in, v))
    copies = [
        pltpu.make_async_copy(source, target, sems.at[i])
        for i, (source, target) in enumerate(pairs)
    ]
    for copy in copies:
        copy.start()
    width = q.shape[1]
    for copy in copies[:3]:
        copy.wait()
    logits = bias[...] + dot_nt(gate[:, width : 2 * width], k[...])
    turned = turn(k, updates[0].shape[1], groups)
    copies[3].wait()
    logits = logits + dot_nt(gate[:, :width], q[...])
    copies[4].wait()
    logits = logits + dot_nt(gate[:, 2 * width :], v[...])
    logits_ref[...] = logits

    def run():
        add_updates(turned, v, cumulate(logits), groups, updates)

    if slots > 2:
        run()
        return
    opening = lax.axis_index("seq") == 0
    pl.when(opening)(run)

    @pl.when(jnp.logical_not(opening))
    def _():
        for update in updates:
            update[...] = jnp.zeros(update.shape, update.dtype)


def within_kernel(heads, groups, q, k, v, logits, resets, cum_ref, attn_ref, within, rise_ref, *updates):
    cum = cumulate(logits[...])
    cum_ref[...] = cum
    rise_ref[...] = (1 - resets[...]).astype(F32) * jnp.exp(cum)
    size = q.shape[1] // heads
    if groups:
        add_updates(turn(k, size, groups), v, cum, groups, updates)
    cum_columns = cum.T
    step = min(heads, STAGE)
    for first in range(0, heads, step):
        count = min(step, heads - first)
        parts = head_lanes(size, first, count)
        scores = [dot_nt(q[:, p], k[:, p]) for p in parts]
        attns = [
            (decay_matrix(cum_columns[:, h : h + 1], cum[h : h + 1, :]) * s).astype(BF16)
            for h, s in enumerate(scores, first)
        ]
        for h, a in enumerate(attns, first):
            attn_ref[h] = a
        for a, p in zip(attns, parts):
            within[:, p] = dot_nn(a, v[:, p])


def mix_kernel(first, count, q, within, cot, rise_ref, state, *refs):
    *forwarded, out, d_mix, pushed, row_ref = refs
    size = state.shape[1]
    opening = lax.axis_index("seq") == 0
    parts, owns = head_lanes(size, first, count), head_lanes(size, 0, count)
    rise = rise_ref[...][first : first + count]
    decays = jnp.where(opening, 0.0, rise).T
    reads = [dot_nn(q[:, p], state[i]) for i, p in enumerate(parts)]
    mixtures = [
        within[:, p] + decays[:, i : i + 1] * x for i, (p, x) in enumerate(zip(parts, reads))
    ]
    upstream = [cot[:, p].astype(F32) for p in parts]
    squares = [jnp.mean(m * m, axis=1, keepdims=True) + EPSILON for m in mixtures]
    shared = [jnp.mean(u * m, axis=1, keepdims=True) for u, m in zip(upstream, mixtures)]
    inverses = [lax.rsqrt(s) for s in squares]
    normed = [m * i for m, i in zip(mixtures, inverses)]
    for n, o in zip(normed, owns):
        out[:, o] = n.astype(BF16)
    grads = [
        ((u - n * (s * i)) * i).astype(BF16)
        for u, n, s, i in zip(upstream, normed, shared, inverses)
    ]
    for g, o in zip(grads, owns):
        d_mix[:, o] = g
    faded = [
        (q[:, p].astype(F32).T * rise[i : i + 1, :]).astype(BF16) for i, p in enumerate(parts)
    ]
    products = [dot_nn(f, g) for f, g in zip(faded, grads)]
    for i, product in enumerate(products):
        product = product.astype(BF16)
        if forwarded:
            product = jnp.where(opening, forwarded[0][i], product)
        pushed[i] = product
    terms = [
        jnp.sum(g.astype(F32) * m, axis=1, keepdims=True) for g, m in zip(grads, mixtures)
    ]
    row_ref[...] = jnp.concatenate(terms, axis=1).T


def members(groups):
    return [(g, i) for g, (_, count) in enumerate(groups) for i in range(count)]


def fading_rows(cum, slots):
    closing = lax.axis_index("seq") == slots - 1
    return jnp.where(closing, 0.0, jnp.exp(cum[:, cum.shape[1] - 1 :] - cum))


def state_terms(keys, moved, fading):
    sums = [jnp.sum(x.astype(F32) * m, axis=1, keepdims=True) for x, m in zip(keys, moved)]
    from_state = jnp.concatenate(sums, axis=1).T * fading
    last = lax.broadcasted_iota(jnp.int32, fading.shape, 1) == fading.shape[1] - 1
    total = jnp.sum(from_state, axis=1, keepdims=True)
    return jnp.where(last, total, 0.0) - from_state


def back_kernel(groups, early, slots, *refs):
    q, k, v, attn, cum_ref, rise_ref = refs[:6]
    number = len(groups)
    outs, d_mixes, states, row_terms = [refs[6 + number * i : 6 + number * (i + 1)] for i in range(4)]
    *grads, output, gq, gk, gv, term_ref, sems = refs[6 + 4 * number :]
    size = states[0].shape[1]
    copies = [
        pltpu.make_async_copy(
            out, output.at[:, pl.ds(first * size, count * size)], sems.at[i]
        )
        for i, ((first, count), out) in enumerate(zip(groups, outs))
    ]
    for copy in copies:
        copy.start()
    cum = cum_ref[...]
    cum_columns = cum.T
    rise_columns = jnp.where(lax.axis_index("seq") == 0, 0.0, rise_ref[...]).T
    fading = fading_rows(cum, slots)
    fading_columns = fading.T
    sums, added = [], []
    places = members(groups)
    for start in range(0, len(places), STAGE):
        some = places[start : start + STAGE]
        heads = range(start, start + len(some))
        parts = head_lanes(size, start, len(some))
        d_outs = [d_mixes[g][:, i * size : (i + 1) * size] for g, i in some]
        columns = [cum_columns[:, h : h + 1] for h in heads]
        d_attns = [dot_nt(d, v[:, p]) for d, p in zip(d_outs, parts)]
        reads = [dot_nt(d, states[g][i]) for d, (g, i) in zip(d_outs, some)]
        weighted = [
            (decay_matrix(c, cum_ref[h : h + 1, :]) * d).astype(BF16)
            for h, c, d in zip(heads, columns, d_attns)
        ]
        ready = [(h, p, g, i) for h, p, (g, i) in zip(heads, parts, some) if g < early]
        moved_k = {h: dot_nt(v[:, p], grads[g][i]) for h, p, g, i in ready}
        moved_v = {h: dot_nn(k[:, p], grads[g][i]) for h, p, g, i in ready}
        for h, p, w, x in zip(heads, parts, weighted, reads):
            gq[:, p] = dot_nn(w, k[:, p]) + rise_columns[:, h : h + 1] * x
        for h, p, w in zip(heads, parts, weighted):
            total = dot_tn(w, q[:, p])
            gk[:, p] = total + fading_columns[:, h : h + 1] * moved_k[h] if h in moved_k else total
        for h, p, d in zip(heads, parts, d_outs):
            total = dot_tn(attn[h], d)
            gv[:, p] = total + fading_columns[:, h : h + 1] * moved_v[h] if h in moved_v else total
        for h, d in zip(heads, d_attns):
            sums.append(jnp.sum(attn[h].astype(F32) * d, axis=0, keepdims=True))
        if ready:
            first = ready[0][0]
            keys = [k[:, p] for _, p, _, _ in ready]
            some_fading = fading[first : first + len(ready)]
            added.append(state_terms(keys, [moved_k[h] for h, *_ in ready], some_fading))
    terms = jnp.concatenate([r[...] for r in row_terms], axis=0) - jnp.concatenate(sums, axis=0)
    if added:
        early_terms = jnp.concatenate(added, axis=0)
        count = early_terms.shape[0]
        term_ref[:count, :] = terms[:count] + early_terms
        term_ref[count:, :] = terms[count:]
    else:
        term_ref[...] = terms
    for copy in copies:
        copy.wait()


def logit_kernel(groups, early, slots, q, k, v, cum_ref, logits_ref, terms, *refs):
    late = len(groups) - early
    through, refs = (refs[0], refs[1:]) if slots > 2 else (None, refs)
    grads, (d_ref, *outs) = refs[:late], refs[late:]
    size = grads[0].shape[1]
    width = q.shape[1]
    cum = cum_ref[...]
    tokens = cum.shape[1]
    first = groups[early][0]
    parts = head_lanes(size, first, cum.shape[0] - first)
    moved = [dot_nt(v[:, p], grads[g][i]) for p, (g, i) in zip(parts, members(groups[early:]))]
    added = state_terms([k[:, p] for p in parts], moved, fading_rows(cum, slots)[first:])
    d_cum = terms[...] if through is None else terms[...] + through[...]
    d_cum = jnp.concatenate([d_cum[:first], d_cum[first:] + added], axis=0) if first else d_cum + added
    d_decay = exact_dot(d_cum, triangle(tokens, False))
    d_logits = (-jax.nn.sigmoid(logits_ref[...]) * d_decay).astype(BF16)
    d_ref[...] = d_logits
    whole = [dot_nn(d_logits, x[...]) for x in (q, k, v)]
    if len(outs) == 1:
        for i in range(3):
            outs[0][:, i * width : (i + 1) * width] = whole[i]
        return
    keep, send, pieces = outs
    joined = jnp.concatenate(whole, axis=1)
    cores, others = pieces.shape[:2]
    piece = 3 * width // (cores * others)
    packed = pack(joined, piece, cores * others)
    for j in range(others):
        for c in range(cores):
            slot, pair = j // (others // slots), j % (others // slots)
            row = pair * cores + c
            pieces[c, j] = packed[row * slots + slot]
    core = lax.axis_index("core")
    keep[...] = pieces[core]
    send[...] = pieces[1 - core]


def pack(joined, piece, count):
    heads, width = joined.shape
    half = heads // 2
    low = lax.broadcasted_iota(jnp.int32, (half, 128), 1) < 64
    behind = pltpu.roll(joined, width - 64, axis=1)
    ahead = pltpu.roll(joined, 64, axis=1)
    packed = []
    for i in range(count):
        at = i * piece // 128 * 128
        source, other = (joined, ahead) if i * piece == at else (behind, joined)
        tiles = [source[:, at + n : at + n + 128] for n in range(0, piece - 127, 128)]
        if piece % 128:
            at += piece // 128 * 128
            lower, upper = source[:half, at : at + 128], other[half:, at : at + 128]
            tiles.append(jnp.where(low, lower, upper))
        packed.append(jnp.concatenate(tiles, axis=0).astype(BF16))
    return packed


def sum_kernel(arrived, out):
    heads, piece = out.shape
    total = jnp.sum(arrived[...].astype(F32), axis=0)
    tiles = piece // 128
    for i in range(tiles):
        out[:, i * 128 : (i + 1) * 128] = total[i * heads : (i + 1) * heads]
    if piece % 128:
        rest = total[tiles * heads :]
        out[: heads // 2, tiles * 128 :] = rest[:, :64]
        out[heads // 2 :, tiles * 128 :] = rest[:, 64:]


def finish_kernel(groups, early, slots, gq, gk, gv, k, v, cum_ref, d_logits, gate, *refs):
    late = len(groups) - early
    grads, outs, (result, sems) = refs[:late], refs[late : late + 3], refs[late + 3 :]
    width = gq.shape[1]
    places = members(groups)
    size = width // len(places)
    fading = fading_rows(cum_ref[...], slots).T
    copies = []
    for index, (partial, operand) in enumerate(((gq, None), (gk, v), (gv, k))):
        for start in range(0, len(places), STAGE):
            some = places[start : start + STAGE]
            at = index * width + start * size
            back = dot_tn(d_logits[...], gate[:, at : at + len(some) * size])
            parts, owns = head_lanes(size, start, len(some)), head_lanes(size, 0, len(some))
            moved = {}
            for h, (p, (g, i)) in enumerate(zip(parts, some), start):
                if operand is not None and g >= early:
                    dot = dot_nt if index == 1 else dot_nn
                    moved[h] = dot(operand[:, p], grads[g - early][i])
            for h, (p, o) in enumerate(zip(parts, owns), start):
                total = partial[:, p] + back[:, o]
                if h in moved:
                    total = total + fading[:, h : h + 1] * moved[h]
                result[index, :, p] = total.astype(BF16)
            lanes = pl.ds(start * size, len(some) * size)
            copies.append(
                pltpu.make_async_copy(
                    result.at[index, :, lanes], outs[index].at[:, lanes], sems.at[len(copies)]
                )
            )
            copies[-1].start()
    for copy in copies:
        copy.wait()


def shape(dims, dtype):
    return jax.ShapeDtypeStruct(dims, dtype)


def head_groups(heads):
    half = heads // 2
    sizes = [half // 3 + (1 if i < half % 3 else 0) for i in range(3)] * 2
    return [(sum(sizes[:i]), size) for i, size in enumerate(sizes)]


def body(
    pairs, cores, seq_size, queries, keys, values, decay_bias, gate_matrix, resets, cotangent
):
    q, k, v, cot = queries[0], keys[0], values[0], cotangent[0]
    tokens, width = q.shape
    heads = decay_bias.shape[1]
    size = width // heads
    gate = gate_matrix.T
    groups = head_groups(heads)
    forward = [(i, i + 1) for i in range(seq_size - 1)]
    backward = [(i + 1, i) for i in range(seq_size - 1)]
    kept = (1 - resets[0, 0]).astype(F32)

    def state_shapes(some):
        return tuple(shape((count, size, size), BF16) for _, count in some)

    ahead = 3 if seq_size == 2 and len(groups) > 2 else len(groups)
    logits, *updates = pl.pallas_call(
        functools.partial(gate_kernel, groups[:ahead], seq_size),
        out_shape=(shape((heads, tokens), F32),) + state_shapes(groups[:ahead]),
        in_specs=[hbm()] * 5,
        out_specs=(spec(),) * (1 + ahead),
        scratch_shapes=[
            pltpu.VMEM((tokens, width), BF16),
            pltpu.VMEM((tokens, width), BF16),
            pltpu.VMEM((tokens, width), BF16),
            pltpu.VMEM((heads, tokens), F32),
            pltpu.VMEM((heads, 3 * width), BF16),
            pltpu.SemaphoreType.DMA((5,)),
        ],
        compiler_params=params(VMEM_FULL),
        cost_estimate=cost(),
        name="gate",
    )(q, k, v, decay_bias[0], gate)
    cum, attn, within, rise, *made = pl.pallas_call(
        functools.partial(within_kernel, heads, groups[ahead:]),
        out_shape=(
            shape((heads, tokens), F32),
            shape((heads, tokens, tokens), BF16),
            shape((tokens, width), F32),
            shape((heads, tokens), F32),
        )
        + state_shapes(groups[ahead:]),
        in_specs=[spec()] * 5,
        out_specs=(spec(),) * (4 + len(groups) - ahead),
        compiler_params=params(),
        cost_estimate=cost(),
        name="within",
    )(q, k, v, logits, resets)
    updates += made

    def chain(own, first, count, pairs):
        if seq_size == 2:
            return lax.ppermute(own, "seq", [(0, 1), (1, 0)])
        arrived = lax.ppermute(own, "seq", pairs)
        for _ in range(seq_size - 2):
            factor = kept * jnp.exp(cum[first : first + count, -1])[:, None, None]
            passed = factor * arrived.astype(F32) + own.astype(F32)
            arrived = lax.ppermute(passed.astype(BF16), "seq", pairs)
        return arrived

    entering = [chain(updates[g], *groups[g], forward) for g in range(ahead)]
    outs, d_mixes, rows, grads = [], [], [], []
    for g, (first, count) in enumerate(groups):
        forwarded = [updates[g + ahead]] if g + ahead < len(groups) else []
        out_g, d_g, pushed, rows_g = pl.pallas_call(
            functools.partial(mix_kernel, first, count),
            out_shape=(
                shape((tokens, count * size), BF16),
                shape((tokens, count * size), BF16),
                shape((count, size, size), BF16),
                shape((count, tokens), F32),
            ),
            in_specs=[spec()] * (5 + len(forwarded)),
            out_specs=(spec(),) * 4,
            compiler_params=params(),
            cost_estimate=cost(),
            name="mix",
        )(q, within, cot, rise, entering[g], *forwarded)
        outs.append(out_g)
        d_mixes.append(d_g)
        rows.append(rows_g)
        if forwarded:
            arrived = lax.ppermute(pushed, "seq", [(0, 1), (1, 0)])
            entering.append(arrived)
            grads.append(arrived)
        else:
            grads.append(chain(pushed, first, count, backward))

    early = min(ahead, len(groups) // 2)
    output, gq, gk, gv, terms = pl.pallas_call(
        functools.partial(back_kernel, groups, early, seq_size),
        out_shape=(shape((tokens, width), BF16),)
        + (shape((tokens, width), F32),) * 3
        + (shape((heads, tokens), F32),),
        in_specs=[spec()] * (6 + 4 * len(groups) + early),
        out_specs=(hbm(),) + (spec(),) * 4,
        scratch_shapes=[pltpu.SemaphoreType.DMA((len(groups),))],
        compiler_params=params(),
        cost_estimate=cost(),
        name="back",
    )(q, k, v, attn, cum, rise, *outs, *d_mixes, *entering, *rows, *grads[:early])
    through = []
    if seq_size > 2:
        products = [
            kept * jnp.sum(g.astype(F32) * s.astype(F32), axis=(1, 2))[:, None]
            for g, s in zip(grads, entering)
        ]
        ends = jnp.concatenate(products, axis=0) * jnp.exp(cum[:, -1:])
        through = [ends * (jnp.arange(tokens) == tokens - 1).astype(F32)]

    piece = 3 * width // (pairs * CORES * seq_size)
    exchanged = cores == CORES and piece >= 128 and piece % 64 == 0 and heads % 16 == 0
    others = pairs * seq_size
    packed = piece * heads // 128
    if exchanged:
        part_shapes = (shape((others, packed, 128), BF16),) * 2
        scratch = [pltpu.VMEM((CORES, others, packed, 128), BF16)]
    else:
        part_shapes = (shape((heads, 3 * width), F32),)
        scratch = []
    d_logits, *parts = pl.pallas_call(
        functools.partial(logit_kernel, groups, early, seq_size),
        out_shape=(shape((heads, tokens), BF16),) + part_shapes,
        in_specs=[spec()] * (6 + len(through) + len(groups) - early),
        out_specs=(spec(),) * (1 + len(part_shapes)),
        scratch_shapes=scratch,
        compiler_params=params(),
        cost_estimate=cost(),
        name="logits",
    )(q, k, v, cum, logits, terms, *through, *grads[early:])

    input_grads = pl.pallas_call(
        functools.partial(finish_kernel, groups, early, seq_size),
        out_shape=(shape((tokens, width), BF16),) * 3,
        in_specs=[spec()] * (8 + len(groups) - early),
        out_specs=(hbm(),) * 3,
        scratch_shapes=[
            pltpu.VMEM((3, tokens, width), BF16),
            pltpu.SemaphoreType.DMA((3 * -(-heads // STAGE),)),
        ],
        compiler_params=params(),
        cost_estimate=cost(),
        name="finish",
    )(gq, gk, gv, k, v, cum, d_logits, gate, *grads[early:])

    if exchanged:
        keep, send = parts
        arrived = lax.ppermute(send, "core", [(0, 1), (1, 0)])
        total = (keep.astype(F32) + arrived.astype(F32)).astype(BF16)
        total, *input_grads = lax.optimization_barrier((total, *input_grads))
        arrived = lax.all_to_all(total, ("seq", "pair"), 0, 0, tiled=True)
        grad_gate = pl.pallas_call(
            sum_kernel,
            out_shape=shape((heads, piece), F32),
            in_specs=[spec()],
            out_specs=spec(),
            compiler_params=params(),
            name="sum",
        )(arrived).T
    else:
        grad_gate = lax.psum_scatter(
            parts[0].T, ("pair", "core", "seq"), scatter_dimension=0, tiled=True
        )
    return output[None], *[g[None] for g in input_grads], grad_gate


def solution(mesh):
    rows, slots = mesh.devices.shape
    cores = CORES if rows % CORES == 0 else 1
    devices = mesh.devices.reshape(rows // cores, cores, slots)
    mesh = jax.sharding.Mesh(devices, ("pair", "core", "seq"))
    row = ("pair", "core")
    tokens = P(row, "seq", None)
    return jax.shard_map(
        functools.partial(body, rows // cores, cores, slots),
        mesh=mesh,
        in_specs=(tokens, tokens, tokens, P(row, None, "seq"), P(), P(row, "seq"), tokens),
        out_specs=(tokens, tokens, tokens, tokens, P((*row, "seq"), None)),
        check_vma=False,
    )
```
